32 devices in a mesh: stream: 2 (over core), dp: 16 (over z, y, x).
Axes of the slice: x: 2, y: 2, z: 4, core: 2. Of those that a mesh axis runs over, the one named last changes fastest.
Arguments:
- frames: bfloat16 [256, 13, 13, 512], P(('stream', 'dp')), parts along dimension 0, may hold values from -6 to 6
- cotangent: bfloat16 [256, 13, 13, 512], P(('stream', 'dp')), parts along dimension 0, may hold values from -6 to 6
- clip_counts: int32 [64], P(('stream', 'dp')), parts along dimension 0, may hold values from 0 to 4, as said below
- conv4_weight: float32 [9216, 512], P(('stream', 'dp')), parts along dimension 0, may hold values from -0.09375 to 0.09375
- conv5_weight: float32 [9216, 512], P(('stream', 'dp')), parts along dimension 0, may hold values from -0.09375 to 0.09375
- biases: float32 [1024, 2], P(('stream', 'dp')), parts along dimension 0, may hold values from -1.5 to 1.5
- conv4_momentum: float32 [9216, 512], P(('stream', 'dp')), parts along dimension 0, may hold values from -4429.9605 to 4429.9605
- conv5_momentum: float32 [9216, 512], P(('stream', 'dp')), parts along dimension 0, may hold values from -4429.9605 to 4429.9605
- bias_momentum: float32 [1024, 2], P(('stream', 'dp')), parts along dimension 0, may hold values from -384 to 384
Outputs:
- outputs: bfloat16 [256, 13, 13, 512], P(('stream', 'dp')), parts along dimension 0
- input_grad: bfloat16 [256, 13, 13, 512], P(('stream', 'dp')), parts along dimension 0
- conv4_moment: float32 [9216, 512], P(('stream', 'dp')), parts along dimension 0
- conv5_moment: float32 [9216, 512], P(('stream', 'dp')), parts along dimension 0
- conv4_new: float32 [9216, 512], P(('stream', 'dp')), parts along dimension 0
- conv5_new: float32 [9216, 512], P(('stream', 'dp')), parts along dimension 0
- conv4_copy: bfloat16 [9216, 512], P(('stream', 'dp')), parts along dimension 0
- conv5_copy: bfloat16 [9216, 512], P(('stream', 'dp')), parts along dimension 0
- bias_moment: float32 [1024, 2], P(('stream', 'dp')), parts along dimension 0
- bias_new: float32 [1024, 2], P(('stream', 'dp')), parts along dimension 0
The draws below stay inside these ranges and needn't reach their ends.
There are 2 independent parts, one for each index of `stream`. The reference program is written for one: setup_inputs(seed, part) draws one part's arguments, and reference() takes and returns one part's arrays. A program takes and returns all parts, laid end to end along the dimension named above; each array names one. Nothing has to cross between parts.
Inputs may be any that keep to these rules, and one draw needn't show every extreme that they name: `clip_counts`: device d of dp holds video slots 2d and 2d + 1; its frame slots hold the first video's clips, then the second's, then empty slots. The two counts of one device sum to at most 8, and some device is full; 0 is an empty video slot.
All inputs are finite; a program needn't handle non-finite values.
Results may differ from the reference program's by a relative error of at most 0.0083.
Values may be sent and summed in bfloat16 or wider, within the bound.
No kernel may reach another device: no remote copies, remote signals or barrier semaphores. Data moves between devices by JAX's collectives and lax.ppermute only.
A program may use at most 256 MiB of HBM per device.

```python
import jax
import jax.numpy as jnp
from jax import lax

C = 512
MAP = 13
FR_DEV = 8
NS_STEPS = 5
K = 4608
CLIPS = 4
FRAMES = 128
N_DP = 16


def draw_clip_counts(key, part):
    key = jax.random.fold_in(key, 7)
    first_key, second_key = jax.random.split(key)
    device = jnp.arange(N_DP, dtype=jnp.int32)
    lowest = 1 + (CLIPS - 1) * device // max(N_DP - 1, 1)
    raw = jax.random.randint(first_key, (N_DP, 2), 0, CLIPS + 1)
    counts = lowest[:, None] + raw % (CLIPS - lowest[:, None] + 1)
    drop = jax.random.randint(second_key, (N_DP,), 0, 2)
    second = jnp.where((drop == 1) & (device < N_DP // 2), 0, counts[:, 1])
    whole = jnp.stack([counts[:, 0], second], axis=1)
    return whole.reshape(-1).astype(jnp.int32)


def rising_rows(key, base, top):
    rows = jnp.arange(K, dtype=jnp.float32) / max(K - 1, 1)
    factor = 1.0 + (top - 1.0) * rows
    noise = jnp.clip(jax.random.normal(key, (K, C), jnp.float32), -6.0, 6.0)
    return (base * factor[:, None] * noise).astype(jnp.float32)


def draw_conv4_momentum(key, part):
    key = jax.random.fold_in(key, 11)
    base = 0.4 * (N_DP * FR_DEV * (MAP * MAP * 0.7)) ** 0.5
    return rising_rows(key, base, 4.0)


def draw_conv5_momentum(key, part):
    key = jax.random.fold_in(key, 13)
    base = 0.3 * (N_DP * FR_DEV * (MAP * MAP * 0.7)) ** 0.5
    return rising_rows(key, base, 4.0)


def levels(own_key, dims, pieces, least, top_value):
    factor_of = 1.0
    for axis_at, shards_of in pieces:
        steps = jax.random.uniform(jax.random.fold_in(jax.random.fold_in(own_key, 6), axis_at), (shards_of,), jnp.float32, least / len(pieces), top_value / len(pieces))
        factor_of = factor_of * jnp.repeat(jnp.exp(steps), dims[axis_at] // shards_of).reshape((-1,) + (1,) * (len(dims) - 1 - axis_at))
    return factor_of


def gaussian(rng, shape, scale, most, cuts=(), kind=jnp.bfloat16):
    values = jax.random.normal(rng, shape, jnp.float32) * scale
    if len(cuts) > 0:
        values = levels(rng, shape, cuts, -0.22, 0.18) * values
    return jnp.clip(values, min=-most, max=most).astype(kind)


def setup_inputs(seed: int = 0, part: int = 0) -> dict:
    splits = jax.random.split(jax.random.key(seed), 10)
    part_keys = jax.random.split(jax.random.fold_in(splits[9], part), 10)
    return {
        "frames": gaussian(part_keys[0], (FRAMES, MAP, MAP, C), 1.0, 6.0, ((0, 16),)),
        "cotangent": gaussian(part_keys[1], (FRAMES, MAP, MAP, C), 1.0, 6.0, ((0, 16),)),
        "clip_counts": draw_clip_counts(jax.random.fold_in(jax.random.fold_in(splits[9], part), 71), part),
        "conv4_weight": gaussian(part_keys[3], (K, C), K ** -0.5, 0.09375, ((0, 16),), jnp.float32),
        "conv5_weight": gaussian(part_keys[4], (K, C), K ** -0.5, 0.09375, ((0, 16),), jnp.float32),
        "biases": gaussian(part_keys[5], (C, 2), 0.3, 1.5, ((0, 16),), jnp.float32),
        "conv4_momentum": draw_conv4_momentum(jax.random.fold_in(jax.random.fold_in(splits[9], part), 71), part),
        "conv5_momentum": draw_conv5_momentum(jax.random.fold_in(jax.random.fold_in(splits[9], part), 71), part),
        "bias_momentum": gaussian(part_keys[8], (C, 2), (0.5 * (N_DP * FR_DEV * (MAP * MAP * 0.7)) ** 0.5), 384.0, ((0, 16),), jnp.float32),
    }


@jax.custom_vjp
def low(v):
    return lax.optimization_barrier(v.astype(jnp.bfloat16)).astype(jnp.float32)

@jax.custom_vjp
def low_back(v):
    return v

def low_keep(v):
    return (low(v), None)

def low_pass(kept, grad):
    return (grad,)

def back_keep(v):
    return (v, None)

def back_low(kept, grad):
    return (low(grad),)
low.defvjp(low_keep, low_pass)
low_back.defvjp(back_keep, back_low)

def activate(value):
    return jax.nn.gelu(value, approximate=True)

def patches(field):
    padded = jnp.pad(field, ((0, 0), (1, 1), (1, 1), (0, 0)))
    taps = [padded[:, r:r + MAP, s:s + MAP, :] for r in range(3) for s in range(3)]
    return jnp.concatenate(taps, axis=-1).reshape(-1, K)

def convolve(field, weight):
    return jnp.dot(patches(field), weight, preferred_element_type=jnp.float32, precision=lax.Precision.HIGHEST)

def forward(inputs, weight4, weight5, bias):
    low4 = low(weight4)
    low5 = low(weight5)
    low_bias = low(bias)

    @jax.checkpoint
    def block(field):
        count = field.shape[0]
        first = low_back(convolve(field, low4) + low_bias[:, 0])
        hidden = low(activate(first)).reshape(count, MAP, MAP, C)
        second = low_back(convolve(hidden, low5) + low_bias[:, 1])
        return activate(second).reshape(count, MAP, MAP, C)
    return lax.map(block, inputs)

def orthogonal(update):
    highest = lax.Precision.HIGHEST
    iterate = update / (jnp.sqrt(jnp.sum(update * update)) + 1e-07)
    for step in range(NS_STEPS):
        gram = jnp.dot(iterate.T, iterate, precision=highest)
        poly = -4.775 * gram + 2.0315 * jnp.dot(gram, gram, precision=highest)
        iterate = 3.4445 * iterate + jnp.dot(iterate, poly, precision=highest)
    return iterate

def reference(frames, cotangent, clip_counts, conv4_weight, conv5_weight, biases, conv4_momentum, conv5_momentum, bias_momentum):
    inputs = frames.astype(jnp.float32).reshape(N_DP, FR_DEV, MAP, MAP, C)
    result, pull = jax.vjp(forward, inputs, conv4_weight, conv5_weight, biases)
    live = lax.optimization_barrier(jnp.sum(clip_counts.reshape(N_DP, 2), axis=1))
    slots = jnp.arange(FR_DEV, dtype=jnp.int32)
    mask = (slots[None, :] < live[:, None]).astype(jnp.float32)
    upstream = cotangent.astype(jnp.float32).reshape(N_DP, FR_DEV, MAP, MAP, C) * mask[:, :, None, None, None]
    back_in, grad4, grad5, grad_bias = pull(upstream)
    outputs = result.reshape(FRAMES, MAP, MAP, C).astype(jnp.bfloat16)
    input_grad = back_in.reshape(FRAMES, MAP, MAP, C).astype(jnp.bfloat16)
    moment4 = 0.5 * conv4_momentum + grad4
    moment5 = 0.5 * conv5_momentum + grad5
    new4 = conv4_weight - orthogonal(grad4 + 0.5 * moment4)
    new5 = conv5_weight - orthogonal(grad5 + 0.5 * moment5)
    bias_moment = 0.5 * bias_momentum + grad_bias
    bias_new = biases - 0.001 * (grad_bias + 0.5 * bias_moment)
    return (outputs, input_grad, moment4, moment5, new4, new5, new4.astype(jnp.bfloat16), new5.astype(jnp.bfloat16), bias_moment, bias_new)
```

```python
import functools
import math

import jax
import jax.numpy as jnp
from jax import lax
from jax.experimental import pallas as pl
from jax.experimental.pallas import tpu as pltpu
from jax.sharding import PartitionSpec as P

NS_STEPS = 5
BF = jnp.bfloat16
F32 = jnp.float32


def split_three(n):
    c = max(d for d in range(1, n + 1) if n % d == 0 and d**3 <= n)
    rest = n // c
    b = max(d for d in range(1, rest + 1) if rest % d == 0 and d**2 <= rest)
    return rest // b, b, c


def shift_pairs(dims, axis, step):
    pairs = []
    for index in range(math.prod(dims)):
        place = [index // (dims[1] * dims[2]), index // dims[2] % dims[1], index % dims[2]]
        place[axis] = (place[axis] + step) % dims[axis]
        pairs.append((index, (place[0] * dims[1] + place[1]) * dims[2] + place[2]))
    return pairs


class Group:
    def __init__(self, n):
        self.dims = split_three(n)
        me = lax.axis_index("dp")
        self.place = (me // (self.dims[1] * self.dims[2]), me // self.dims[2] % self.dims[1], me % self.dims[2])

    def spread(self, block, axis):
        size = self.dims[axis]
        got = [block]
        for j in range(1, size):
            got.append(lax.ppermute(block, "dp", shift_pairs(self.dims, axis, -j)))
        return jnp.stack(got)

    def settle(self, stack, at, axis):
        return jnp.roll(stack, self.place[axis], axis=at)

    def gather(self, block):
        rows, cols = block.shape
        half = rows // 2
        near = self.spread(block, 0)
        one = self.spread(self.spread(near[:, :half], 2), 1)
        two = self.spread(self.spread(near[:, half:], 1), 2)
        one = jnp.transpose(one, (2, 0, 1, 3, 4))
        two = jnp.transpose(two, (2, 1, 0, 3, 4))
        whole = jnp.concatenate([one, two], axis=3)
        for axis in range(3):
            whole = self.settle(whole, axis, axis)
        return whole.reshape(-1, cols)

    def gather_small(self, block):
        got = self.spread(self.spread(self.spread(block, 0), 1), 2)
        got = jnp.moveaxis(got, (0, 1, 2), (2, 1, 0))
        for axis in range(3):
            got = self.settle(got, axis, axis)
        return got.reshape((-1,) + block.shape[1:])

    def fold(self, parts, at, axis, kind):
        size = self.dims[axis]
        total = lax.dynamic_index_in_dim(parts, self.place[axis], at, keepdims=False)
        for j in range(1, size):
            out = lax.dynamic_index_in_dim(parts, (self.place[axis] + j) % size, at, keepdims=False)
            got = lax.ppermute(out.astype(kind), "dp", shift_pairs(self.dims, axis, j))
            total = total + got.astype(F32)
        return total

    def scatter_sum(self, whole, kind):
        cols = whole.shape[1]
        parts = whole.reshape(self.dims + (-1, cols))
        half = parts.shape[3] // 2
        one = self.fold(self.fold(parts[:, :, :, :half], 2, 2, kind), 1, 1, kind)
        two = self.fold(self.fold(parts[:, :, :, half:], 1, 1, kind), 1, 2, kind)
        return self.fold(jnp.concatenate([one, two], axis=1), 0, 0, kind)

    def scatter_sum_small(self, whole):
        parts = whole.reshape(self.dims + (-1,) + whole.shape[1:])
        return self.fold(self.fold(self.fold(parts, 2, 2, F32), 1, 1, F32), 0, 0, F32)

    def sum_gram(self, gram):
        half = gram.shape[0] // 2
        packed = jnp.concatenate([gram[:half, :half], gram[:half, half:], gram[half:, half:]], axis=0)
        packed = self.gather(self.scatter_sum(packed, F32))
        corner = packed[half : 2 * half]
        return jnp.concatenate(
            [
                jnp.concatenate([packed[:half], corner], axis=1),
                jnp.concatenate([corner.T, packed[2 * half :]], axis=1),
            ],
            axis=0,
        )


def activate(value):
    return jax.nn.gelu(value, approximate=True)


def convolve(field, weight):
    width = field.shape[3]
    return lax.conv_general_dilated(
        field,
        weight.reshape(3, 3, width, -1),
        (1, 1),
        ((1, 1), (1, 1)),
        dimension_numbers=("NHWC", "HWIO", "NHWC"),
        preferred_element_type=F32,
    )


def convolve_back(delta, weight):
    width = delta.shape[3]
    return lax.conv_general_dilated(
        delta,
        weight.reshape(3, 3, -1, width)[::-1, ::-1],
        (1, 1),
        ((1, 1), (1, 1)),
        dimension_numbers=("NHWC", "HWOI", "NHWC"),
        preferred_element_type=F32,
    )


def weight_gradient(field, delta):
    grad = lax.conv_general_dilated(
        field,
        delta,
        (1, 1),
        ((1, 1), (1, 1)),
        dimension_numbers=("CHWN", "IHWO", "HWNC"),
        preferred_element_type=F32,
    )
    return grad.reshape(-1, delta.shape[3])


def halves(value):
    high = value.astype(BF)
    return high, (value - high.astype(F32)).astype(BF)


def product(left, right):
    dot = functools.partial(jnp.dot, preferred_element_type=F32)
    return dot(left[0], right[0]) + (dot(left[0], right[1]) + dot(left[1], right[0]))


def newton_kernel(gram_ref, update_ref, weight_ref, new_ref, copy_ref):
    gram = gram_ref[...]
    size = gram.shape[0]
    diagonal = lax.broadcasted_iota(jnp.int32, (size, size), 0) == lax.broadcasted_iota(jnp.int32, (size, size), 1)
    square = jnp.sum(jnp.where(diagonal, gram, 0.0))
    scale = 1.0 / (jnp.sqrt(square) + 1e-07)
    gram = gram * scale * scale
    iterate = update_ref[...] * scale
    for step in range(NS_STEPS):
        parts = halves(gram)
        poly = halves(-4.775 * gram + 2.0315 * product(parts, parts))
        iterate = 3.4445 * iterate + product(halves(iterate), poly)
        if step < NS_STEPS - 1:
            middle = 3.4445 * gram + product(parts, poly)
            gram = 3.4445 * middle + product(halves(middle), poly)
    new = weight_ref[...] - iterate
    new_ref[...] = new
    copy_ref[...] = new.astype(BF)


def newton(gram, update, weight):
    return pl.pallas_call(
        newton_kernel,
        out_shape=(jax.ShapeDtypeStruct(weight.shape, F32), jax.ShapeDtypeStruct(weight.shape, BF)),
        compiler_params=pltpu.CompilerParams(vmem_limit_bytes=48 * 1024 * 1024),
        cost_estimate=pl.CostEstimate(flops=100 * 512**3, bytes_accessed=4 * 1024 * 1024, transcendentals=0),
    )(gram, update, weight)


def on_device(
    n_dp,
    frames,
    cotangent,
    clip_counts,
    conv4_weight,
    conv5_weight,
    biases,
    conv4_momentum,
    conv5_momentum,
    bias_momentum,
):
    group = Group(n_dp)
    count, width = (frames.shape[0], frames.shape[3])
    half = width // 2
    bias_full = group.gather_small(biases.astype(BF)).astype(F32)
    low4 = conv4_weight.astype(BF)
    low5 = conv5_weight.astype(BF)
    full4 = [group.gather(low4[:, :half]), group.gather(low4[:, half:])]
    full5 = [group.gather(low5[:, :half]), group.gather(low5[:, half:])]

    first = jnp.concatenate([convolve(frames, full) for full in full4], axis=3) + bias_full[:, 0]
    hidden, pull_first = jax.vjp(activate, first)
    hidden = hidden.astype(BF)
    second = jnp.concatenate([convolve(hidden, full) for full in full5], axis=3) + bias_full[:, 1]
    result, pull_second = jax.vjp(activate, second)
    outputs = result.astype(BF)
    live = jnp.sum(clip_counts)
    mask = (jnp.arange(count, dtype=jnp.int32) < live).astype(F32)
    upstream = cotangent.astype(F32) * mask[:, None, None, None]
    delta_second = pull_second(upstream)[0].astype(BF)
    whole5 = weight_gradient(hidden, delta_second)
    grad5 = jnp.concatenate([group.scatter_sum(whole5[:, :half], BF), group.scatter_sum(whole5[:, half:], BF)], axis=1)
    back_mid = convolve_back(delta_second[..., :half], full5[0]) + convolve_back(delta_second[..., half:], full5[1])
    delta_first = pull_first(back_mid)[0].astype(BF)
    whole4 = weight_gradient(frames, delta_first)
    grad4 = jnp.concatenate([group.scatter_sum(whole4[:, :half], BF), group.scatter_sum(whole4[:, half:], BF)], axis=1)
    back_in = convolve_back(delta_first[..., :half], full4[0]) + convolve_back(delta_first[..., half:], full4[1])
    input_grad = back_in.astype(BF)
    bias_terms = jnp.stack(
        [
            jnp.sum(delta_first.astype(F32), axis=(0, 1, 2)),
            jnp.sum(delta_second.astype(F32), axis=(0, 1, 2)),
        ],
        axis=1,
    )
    grad_bias = group.scatter_sum_small(bias_terms)

    moment5 = 0.5 * conv5_momentum + grad5
    update5 = grad5 + 0.5 * moment5
    moment4 = 0.5 * conv4_momentum + grad4
    update4 = grad4 + 0.5 * moment4

    def gram_of(update):
        low = update.astype(BF)
        return lax.dot_general(low, low, (((0,), (0,)), ((), ())), preferred_element_type=F32)

    new5, copy5 = newton(group.sum_gram(gram_of(update5)), update5, conv5_weight)
    new4, copy4 = newton(group.sum_gram(gram_of(update4)), update4, conv4_weight)
    bias_moment = 0.5 * bias_momentum + grad_bias
    bias_new = biases - 0.001 * (grad_bias + 0.5 * bias_moment)
    return (
        outputs,
        input_grad,
        moment4,
        moment5,
        new4,
        new5,
        copy4,
        copy5,
        bias_moment,
        bias_new,
    )


def solution(mesh):
    rows = P(("stream", "dp"), None)
    field = P(("stream", "dp"), None, None, None)
    return jax.shard_map(
        functools.partial(on_device, mesh.shape["dp"]),
        mesh=mesh,
        in_specs=(field, field, P(("stream", "dp")), rows, rows, rows, rows, rows, rows),
        out_specs=(field, field) + (rows,) * 8,
        check_vma=False,
    )
```

```python
import functools
import math

import jax
import jax.numpy as jnp
from jax import lax
from jax.experimental import pallas as pl
from jax.experimental.pallas import tpu as pltpu
from jax.sharding import PartitionSpec as P

NS_STEPS = 5
BIAS_ROWS = 16
BLOCK = 256
LANES = 128
BF = jnp.bfloat16
F32 = jnp.float32
VMEM = pl.BlockSpec(memory_space=pltpu.VMEM)
SMEM = pl.BlockSpec(memory_space=pltpu.SMEM)
ANY = pl.BlockSpec(memory_space=pl.ANY)
HBM = pl.BlockSpec(memory_space=pltpu.HBM)


def together(*values):
    return lax.optimization_barrier(values)


class Chain:
    def __init__(self):
        self.link = None

    def run(self, kernel, operands, outs, scratch=(), limit=30, need=()):
        before = list(need) + ([] if self.link is None else [self.link])
        n, m = len(operands), len(before)

        def linked(*refs):
            link = refs[n + m + len(outs)]
            kernel(*refs[:n], *refs[n + m : n + m + len(outs)], *refs[n + m + len(outs) + 1 :])
            link[...] = jnp.zeros_like(link)

        result = pl.pallas_call(
            linked,
            in_specs=[spec for spec, _ in operands] + [ANY] * m,
            out_specs=[VMEM] * (len(outs) + 1),
            out_shape=[jax.ShapeDtypeStruct(shape, kind) for shape, kind in outs + [((8, 128), F32)]],
            scratch_shapes=list(scratch),
            compiler_params=pltpu.CompilerParams(vmem_limit_bytes=limit * 1024 * 1024),
            cost_estimate=pl.CostEstimate(flops=1, bytes_accessed=3_000_000, transcendentals=0),
        )(*[array for _, array in operands], *before)
        *results, self.link = result
        return results


def copy_all(pairs, sem):
    copies = [pltpu.make_async_copy(source, target, sem.at[k]) for k, (source, target) in enumerate(pairs)]
    for copy in copies:
        copy.start()
    for copy in copies:
        copy.wait()


class Field:
    def __init__(self, side, count):
        self.side, self.count = side, count
        self.line = (side + 1) * count
        self.cells = side * self.line
        self.lead = -(-self.line // 16) * 16 + 16
        self.rows = -(-(self.lead + self.cells + self.line + count) // 16) * 16

    def tap(self, r, s):
        start = self.lead + (r - 1) * self.line + (s - 1) * self.count
        return (0, start) if start % 16 == 0 else (1, start - self.count)

    def flat(self, values):
        cells = jnp.transpose(values, (1, 2, 0, 3))
        cells = jnp.pad(cells, ((0, 0), (0, 1), (0, 0), (0, 0)))
        return cells.reshape(self.cells, -1)

    def pair(self, flat):
        after = self.rows - self.lead - self.cells
        return (
            jnp.pad(flat, ((self.lead, after), (0, 0))),
            jnp.pad(flat, ((self.lead - self.count, after + self.count), (0, 0))),
        )

    def unflat(self, flat):
        cells = flat.reshape(self.side, self.side + 1, self.count, -1)[:, : self.side]
        return jnp.transpose(cells, (2, 0, 1, 3))

    def sweep(self, wide, pair, columns, body):
        count, lead, line, cells = self.count, self.lead, self.line, self.cells
        width = wide.shape[1]
        pad = jnp.zeros((count, LANES), F32)

        totals = [jnp.zeros((8, LANES), F32)] * (width // LANES)
        for row in range(0, cells, line):
            for c in range(0, width, LANES):
                some = slice(columns.start + c, columns.start + c + LANES)
                value = body(slice(row, row + line), some, wide[row + count : row + count + line, c : c + LANES])
                value = jnp.concatenate([value[: line - count], pad], axis=0)
                low = value.astype(BF)
                pair[0][lead + row : lead + row + line, some] = low
                value = low.astype(F32)
                wide[row + count : row + count + line, c : c + LANES] = value
                totals[c // LANES] = totals[c // LANES] + jnp.sum(value.reshape(line // 8, 8, LANES), axis=0)
        wide[0:count] = jnp.zeros((count, width), F32)
        wide[count + cells :] = jnp.zeros((count, width), F32)
        end = self.rows - lead - cells
        pair[0][0:lead, columns] = jnp.zeros((lead, width), BF)
        pair[0][lead + cells :, columns] = jnp.zeros((end, width), BF)
        pair[1][0 : lead - 16, columns] = jnp.zeros((lead - 16, width), BF)
        pair[1][lead + cells :, columns] = jnp.zeros((end, width), BF)
        pair[1][lead - 16 : lead + cells, columns] = wide[0 : cells + 16, :].astype(BF)
        return jnp.concatenate([jnp.sum(total, axis=0, keepdims=True) for total in totals], axis=1)

    def wide(self):
        return pltpu.VMEM((self.cells + 2 * self.count, BLOCK), F32)


def convolve_block(field, pair, full, columns):
    width = pair[0].shape[1]
    total = None
    for r in range(3):
        for s in range(3):
            which, start = field.tap(r, s)
            tap = (3 * r + s) * width
            part = jnp.dot(
                pair[which][start : start + field.cells, :],
                full[tap : tap + width, columns],
                preferred_element_type=F32,
            )
            total = part if total is None else total + part
    return total


def convolve_back_block(field, pairs, full, at, cols):
    width = full.shape[0] // 9
    total = None
    for r in range(3):
        for s in range(3):
            which, start = field.tap(2 - r, 2 - s)
            tap = (3 * r + s) * width + at
            begin = 0
            for pair in pairs:
                end = begin + pair[0].shape[1]
                part = lax.dot_general(
                    pair[which][start : start + field.cells, :],
                    full[tap : tap + cols, begin:end],
                    (((1,), (1,)), ((), ())),
                    preferred_element_type=F32,
                )
                total = part if total is None else total + part
                begin = end
    return total


def gradient_into(field, pair, delta, out, looped):
    width = pair[0].shape[1]

    def line(r, carry):
        for s in range(3):
            which, start = field.tap(0, s)
            start = start + r * field.line
            tap = (3 * r + s) * width
            if looped:
                start, tap = pl.multiple_of(start, 16), pl.multiple_of(tap, width)
            out[pl.ds(tap, width), :] = lax.dot_general(
                pair[which][pl.ds(start, field.cells), :], delta[...], (((0,), (0,)), ((), ())), preferred_element_type=F32
            )
        return carry

    if looped:
        lax.fori_loop(0, 3, line, 0)
    else:
        for r in range(3):
            line(r, 0)


def activate(value):
    square = value * value
    slope = 0.7978845608
    bend = jnp.tanh(slope * value * (1.0 + 0.044715 * square))
    rise = 0.5 * (1.0 + bend)
    steep = slope * (1.0 + 3 * 0.044715 * square)
    return value * rise, rise + 0.5 * value * (1.0 - bend * bend) * steep


class Weights:
    def __init__(self, total):
        self.total, self.cols = total, 0
        self.arrays, self.plan = [], []

    def add(self, cols, found):
        for part, start, left, height, where in found:
            if not any(other is part for other in self.arrays):
                self.arrays.append(part)
            which = [k for k, other in enumerate(self.arrays) if other is part][0]
            self.plan.append((which, start, left, height, where, self.cols, cols))
        self.cols += cols
        return self

    def operands(self):
        return [(HBM, array) for array in self.arrays]

    def scratch(self, more=0):
        return [pltpu.VMEM((self.total, self.cols), BF), pltpu.SemaphoreType.DMA((len(self.plan) + more,))]

    def copies(self, place, arrays, full):
        return [
            (
                arrays[which].at[pl.ds(start, height), pl.ds(left, cols)],
                full.at[pl.ds(pl.multiple_of(where(place), 16), height), pl.ds(column, cols)],
            )
            for which, start, left, height, where, column, cols in self.plan
        ]


def first_layer(chain, field, place, weights, pair, bias_rows):
    width = weights.cols
    n = len(weights.arrays)
    sources = [([other is array for other in weights.arrays].index(True), row) for array, row in bias_rows]

    def kernel(*refs):
        place_ref, arrays, rest = refs[0], refs[1 : n + 1], refs[n + 1 :]
        even_in, odd_in, out_even, out_odd, slope_ref, bias_ref, even, odd, terms, wide, full, sem = rest
        lines = [
            (arrays[which].at[pl.ds(row, BIAS_ROWS)], terms.at[pl.ds(k * BIAS_ROWS, BIAS_ROWS)])
            for k, (which, row) in enumerate(sources)
        ]
        copy_all(weights.copies(place_ref, arrays, full) + [(even_in, even), (odd_in, odd)] + lines, sem)
        total = terms[0:BIAS_ROWS].astype(F32)
        for k in range(1, len(lines)):
            total = total + terms[k * BIAS_ROWS : (k + 1) * BIAS_ROWS].astype(F32)
        bias_ref[...] = total
        for at in range(0, width, BLOCK):
            columns = slice(at, at + BLOCK)
            wide[field.count : field.count + field.cells] = convolve_block(field, (even, odd), full, columns)

            def body(rows, some, value):
                result, slope_ref[rows, some] = activate(value + bias_ref[0:1, some])
                return result

            field.sweep(wide, (out_even, out_odd), columns, body)

    form = pltpu.VMEM(pair[0].shape, BF)
    terms = pltpu.VMEM((len(sources) * BIAS_ROWS, width), BF)
    return chain.run(
        kernel,
        [(SMEM, place)] + weights.operands() + [(HBM, pair[0]), (HBM, pair[1])],
        [((field.rows, width), BF)] * 2 + [((field.cells, width), F32), ((BIAS_ROWS, width), F32)],
        [form, form, terms, field.wide()] + weights.scratch(2 + len(sources)),
        limit=36,
    )


def second_layer(chain, field, place, weights, pair, bias, upstream, pack, packed, need=()):
    width = weights.cols
    n = len(weights.arrays)

    def kernel(*refs):
        place_ref, arrays, rest = refs[0], refs[1 : n + 1], refs[n + 1 :]
        even_in, odd_in, bias_ref, up_in, out_ref, d_even, d_odd, sum_ref, *outs, even, odd, grad, up_ref, wide, full, sem = rest
        copy_all(weights.copies(place_ref, arrays, full) + [(even_in, even), (odd_in, odd), (up_in, up_ref)], sem)
        wide[field.count : field.count + field.cells] = convolve_block(field, (even, odd), full, slice(0, width))

        def body(rows, some, value):
            result, slope = activate(value + bias_ref[:, some])
            out_ref[rows, some] = result.astype(BF)
            return up_ref[rows, some].astype(F32) * slope

        sum_ref[...] = field.sweep(wide, (d_even, d_odd), slice(0, width), body)
        gradient_into(field, (even, odd), d_even.at[pl.ds(field.lead, field.cells)], grad, True)
        pack(place_ref, grad, outs)

    form = ((field.rows, width), BF)
    form_in = pltpu.VMEM(pair[0].shape, BF)
    return chain.run(
        kernel,
        [(SMEM, place)] + weights.operands() + [(ANY, pair[0]), (ANY, pair[1]), (VMEM, bias), (HBM, upstream)],
        [((field.cells, width), BF), form, form, ((1, width), F32)] + packed,
        [form_in, form_in, pltpu.VMEM((9 * pair[0].shape[1], width), F32), pltpu.VMEM((field.cells, width), BF)]
        + [field.wide()]
        + weights.scratch(3),
        limit=36,
        need=need,
    )


def back_layer(chain, field, place, weights, pairs, slope, need=()):
    width = weights.total // 9
    n = len(weights.arrays)
    flat = [form for pair in pairs for form in pair]

    def kernel(*refs):
        place_ref, arrays, rest = refs[0], refs[1 : n + 1], refs[n + 1 :]
        sources, rest = rest[: len(flat)], rest[len(flat) :]
        slope_in, d_even, d_odd, sum_ref, *deltas, slope_ref, wide, full, sem = rest
        copy_all(weights.copies(place_ref, arrays, full) + list(zip(sources, deltas)) + [(slope_in, slope_ref)], sem)
        held = [deltas[k : k + 2] for k in range(0, len(flat), 2)]
        for at in range(0, width, BLOCK):
            columns = slice(at, at + BLOCK)
            wide[field.count : field.count + field.cells] = convolve_back_block(field, held, full, at, BLOCK)

            def body(rows, some, value):
                return value * slope_ref[rows, some]

            sum_ref[:, columns] = field.sweep(wide, (d_even, d_odd), columns, body)

    return chain.run(
        kernel,
        [(SMEM, place)] + weights.operands() + [(HBM, form) for form in flat[:2]] + [(ANY, form) for form in flat[2:]] + [(HBM, slope)],
        [((field.rows, width), BF)] * 2 + [((1, width), F32)],
        [pltpu.VMEM(form.shape, BF) for form in flat]
        + [pltpu.VMEM(slope.shape, F32), field.wide()]
        + weights.scratch(len(flat) + 1),
        limit=36,
        need=need,
    )


def input_layer(chain, field, place, weights, pair):
    n = len(weights.arrays)
    width = weights.total // 9

    def kernel(*refs):
        place_ref, arrays, rest = refs[0], refs[1 : n + 1], refs[n + 1 :]
        even_in, odd_in, out_ref, even, odd, full, sem = rest
        copy_all(weights.copies(place_ref, arrays, full) + [(even_in, even), (odd_in, odd)], sem)
        for at in range(0, width, BLOCK):
            out_ref[:, at : at + BLOCK] = convolve_back_block(field, [(even, odd)], full, at, BLOCK).astype(BF)

    operands = [(SMEM, place)] + weights.operands() + [(ANY, pair[0]), (ANY, pair[1])]
    form = pltpu.VMEM(pair[0].shape, BF)
    return chain.run(kernel, operands, [((field.cells, width), BF)], [form, form] + weights.scratch(2), limit=30)[0]


def weight_gradient(chain, field, place, pair, delta, at, cols, pack, packed, need=()):
    width = pair[0].shape[1]

    def kernel(place_ref, even_in, odd_in, delta_in, *rest):
        *outs, even, odd, delta_ref, grad, sem = rest
        columns = pl.ds(at, cols)
        copy_all([(even_in, even), (odd_in, odd), (delta_in.at[:, columns], delta_ref)], sem)
        delta = delta_ref.at[pl.ds(field.lead, field.cells)]
        gradient_into(field, (even, odd), delta, grad, False)
        pack(place_ref, grad, outs)

    form = pltpu.VMEM(pair[0].shape, BF)
    return chain.run(
        kernel,
        [(SMEM, place), (HBM, pair[0]), (HBM, pair[1]), (ANY, delta)],
        packed,
        [form, form, pltpu.VMEM((delta.shape[0], cols), BF)]
        + [pltpu.VMEM((9 * width, cols), F32), pltpu.SemaphoreType.DMA((3,))],
        limit=36,
        need=need,
    )


def halves(value):
    high = value.astype(BF)
    return high, (value - high.astype(F32)).astype(BF)


def product(left, right):
    return jnp.dot(
        jnp.concatenate([left[0], left[0], left[1]], axis=1),
        jnp.concatenate([right[0], right[1], right[0]], axis=0),
        preferred_element_type=F32,
    )


def square_masks(size):
    row = lax.broadcasted_iota(jnp.int32, (size, size), 0)
    column = lax.broadcasted_iota(jnp.int32, (size, size), 1)
    return row, column


def gram_into(parts, update, terms, out_ref):
    low = update.astype(BF)
    half = low.shape[1] // 2
    each = 2 * half // parts
    left, right = low[:, :half], low[:, half:]

    def block(one, two):
        return lax.dot_general(one, two, (((0,), (0,)), ((), ())), preferred_element_type=F32)

    row, column = square_masks(half)
    last = block(right, right)
    for k, value in enumerate((block(left, right), jnp.where(column >= row, block(left, left), last))):
        for part in range(parts):
            first = max(part * each, k * half)
            end = min((part + 1) * each, (k + 1) * half)
            if first < end:
                out_ref[part, first - part * each : end - part * each] = value[first - k * half : end - k * half]
    diagonal = jnp.sum(jnp.where(column == row, last, 0.0), axis=0, keepdims=True)
    for part in range(parts):
        out_ref[part, each : each + 1] = terms[part : part + 1]
        out_ref[part, each + 1 : each + 2] = diagonal if part == 0 else jnp.zeros_like(diagonal)
        out_ref[part, each + 2 :] = jnp.zeros((6, half), F32)


def newton_start(order, place_ref, sums, update_ref, packed, below):
    each = packed.shape[0] // len(sums)
    for j, part in enumerate(sums):
        at = order(place_ref, j)
        packed[pl.ds(pl.multiple_of(at * each, 8), each), :] = part[:each]
        below[pl.ds(pl.multiple_of(at * 8, 8), 8), :] = part[each:]
    half = packed.shape[1]
    row, column = square_masks(half)
    corner = packed[:half]
    mixed = packed[half:]
    turned = mixed.T
    last = jnp.where(column < row, mixed, jnp.where(column > row, turned, below[1:2]))
    gram = jnp.concatenate(
        [
            jnp.concatenate([jnp.where(column >= row, mixed, turned), corner], axis=1),
            jnp.concatenate([corner.T, last], axis=1),
        ],
        axis=0,
    )
    square = jnp.sum(jnp.where(column == row, mixed, 0.0)) + jnp.sum(below[1:2])
    scale = 1.0 / (jnp.sqrt(square) + 1e-07)
    return gram * scale * scale, update_ref[...] * scale


def newton_steps(gram, iterate, steps):
    for step in steps:
        parts = halves(gram)
        poly = halves(-4.775 * gram + 2.0315 * product(parts, parts))
        iterate = 3.4445 * iterate + product(halves(iterate), poly)
        if step < NS_STEPS - 1:
            middle = 3.4445 * gram + product(parts, poly)
            gram = 3.4445 * middle + product(halves(middle), poly)
    return gram, iterate


def newton(chain, place, order, sums, update, weight):
    width = weight.shape[1]
    n = len(sums)

    def kernel(place_ref, *refs):
        update_ref, weight_ref, new_ref, copy_ref, packed, below = refs[n:]
        state = newton_start(order, place_ref, refs[:n], update_ref, packed, below)
        new = weight_ref[...] - newton_steps(*state, range(NS_STEPS))[1]
        new_ref[...] = new
        copy_ref[...] = new.astype(BF)

    return chain.run(
        kernel,
        [(SMEM, place)] + [(VMEM, part) for part in sums] + [(VMEM, update), (VMEM, weight)],
        [(weight.shape, F32), (weight.shape, BF)],
        [pltpu.VMEM((width, width // 2), F32), pltpu.VMEM((8 * n, width // 2), F32)],
    )


def newton_first(chain, place, order, sums, update, last):
    width = update.shape[1]
    n = len(sums)

    def kernel(place_ref, *refs):
        update_ref, gram_ref, iterate_ref, packed, below = refs[n:]
        state = newton_start(order, place_ref, refs[:n], update_ref, packed, below)
        gram_ref[...], iterate_ref[...] = newton_steps(*state, range(last))

    return chain.run(
        kernel,
        [(SMEM, place)] + [(VMEM, part) for part in sums] + [(VMEM, update)],
        [((width, width), F32), (update.shape, F32)],
        [pltpu.VMEM((width, width // 2), F32), pltpu.VMEM((8 * n, width // 2), F32)],
    )


def newton_next(chain, state, first, last):
    def kernel(gram_ref, iterate_ref, gram_out, iterate_out):
        gram_out[...], iterate_out[...] = newton_steps(gram_ref[...], iterate_ref[...], range(first, last))

    return chain.run(kernel, [(VMEM, part) for part in state], [(part.shape, F32) for part in state])


def newton_last(chain, state, first, weight):
    def kernel(gram_ref, iterate_ref, weight_ref, new_ref, copy_ref):
        new = weight_ref[...] - newton_steps(gram_ref[...], iterate_ref[...], range(first, NS_STEPS))[1]
        new_ref[...] = new
        copy_ref[...] = new.astype(BF)

    operands = [(VMEM, part) for part in state] + [(VMEM, weight)]
    return chain.run(kernel, operands, [(weight.shape, F32), (weight.shape, BF)])


class Box:
    def __init__(self, chain, n, rows):
        self.chain = chain
        self.depth = n // 4
        self.n, self.rows, self.cut = n, rows, rows // 2
        me = lax.axis_index("dp")
        self.place = jnp.stack([me // 4, me // 2 % 2, me % 2]).astype(jnp.int32)

    def move(self, block, z, y=0, x=0):
        pairs = []
        for index in range(self.n):
            to = ((index // 4 + z) % self.depth) * 4 + ((index // 2 + y) % 2) * 2 + (index + x) % 2
            pairs.append((index, to))
        return lax.ppermute(block, "dp", pairs)

    def deep(self, block):
        return [self.move(block, -j) for j in range(1, self.depth)]

    def swap_deep(self, blocks):
        groups = [[4 * z + k for z in range(self.depth)] for k in range(4)]
        return lax.all_to_all(blocks, "dp", 0, 0, axis_index_groups=groups, tiled=True)

    def owner(self, z, y, x, fixed):
        def where(place):
            at = z if fixed else lax.rem(place[0] + z, self.depth)
            return ((at * 2 + lax.rem(place[1] + y, 2)) * 2 + lax.rem(place[2] + x, 2)) * self.rows

        return where


    def split(self, blocks, parts):
        cut, rows = self.cut, self.rows

        cols = blocks.shape[1] // parts

        def kernel(source, *outs):
            for k in range(parts):
                upper, lower = outs[2 * k : 2 * k + 2]
                columns = slice(k * cols, (k + 1) * cols)
                for j in range(self.depth):
                    upper[j * cut : (j + 1) * cut] = source[j * rows : j * rows + cut, columns]
                    lower[j * (rows - cut) : (j + 1) * (rows - cut)] = source[j * rows + cut : (j + 1) * rows, columns]

        outs = [((self.depth * cut, cols), BF), ((self.depth * (rows - cut), cols), BF)] * parts
        return self.chain.run(kernel, [(VMEM, blocks)], outs)

    def gate(self, arrays):
        def kernel(out):
            out[...] = jnp.zeros_like(out)

        self.chain.run(kernel, [], [((8, 128), F32)], need=arrays)

    def near(self, blocks, need=()):
        cut, tall = self.cut, blocks[0].shape[0]
        low = tall - cut

        def kernel(*refs):
            *sources, upper, lower = refs
            for j, source in enumerate(sources):
                upper[j * cut : (j + 1) * cut] = source[:cut]
                lower[j * low : (j + 1) * low] = source[cut:]

        cols = blocks[0].shape[1]
        outs = [((len(blocks) * cut, cols), BF), ((len(blocks) * low, cols), BF)]
        return self.chain.run(kernel, [(VMEM, block) for block in blocks], outs, need=need)

    def found(self, upper, lower, tall, fixed=False):
        pieces = []
        for at, height, arrays in ((0, tall[0], upper), (self.cut, tall[1], lower)):
            for (y, x), array, first in arrays:
                for z in range(self.depth):
                    where = functools.partial(lambda f, a, p: f(p) + a, self.owner(z, y, x, fixed), at)
                    pieces.append((array, first + z * height // self.depth, 0, self.cut, where))
        return pieces

    def gather_planes(self, upper, lower, x_upper, y_lower, need=()):
        tall = upper.shape[0], lower.shape[0]
        cols = upper.shape[1]

        def kernel(a, a_got, b, b_got, a_wide, b_wide):
            a_wide[: tall[0]], a_wide[tall[0] :] = a[...], a_got[...]
            b_wide[: tall[1]], b_wide[tall[1] :] = b[...], b_got[...]

        operands = [(VMEM, array) for array in (upper, x_upper, lower, y_lower)]
        wide = self.chain.run(kernel, operands, [((2 * height, cols), BF) for height in tall], need=need)
        y_wide, x_wide = self.move(wide[0], 0, 1, 0), self.move(wide[1], 0, 0, 1)
        uppers = [((0, 0), wide[0], 0), ((0, 1), wide[0], tall[0]), ((1, 0), y_wide, 0), ((1, 1), y_wide, tall[0])]
        lowers = [((0, 0), wide[1], 0), ((1, 0), wide[1], tall[1]), ((0, 1), x_wide, 0), ((1, 1), x_wide, tall[1])]
        return uppers, lowers, tall


    def block(self, ref, index, rows):
        return ref[pl.ds(pl.multiple_of(index * rows, 8), rows), :]

    def packed_plane(self, cols):
        tall = 2 * self.depth * self.cut
        return [((tall, cols), BF)] * 4

    def pack_plane(self, place, grad, outs):
        cut = self.cut
        for z in range(self.depth):
            for k in range(2):
                to = slice((2 * z + k) * cut, (2 * z + k + 1) * cut)
                for step in range(2):
                    x = lax.rem(place[2] + step, 2)
                    y = lax.rem(place[1] + step, 2)
                    upper = ((z * 2 + k) * 2 + x) * self.rows
                    lower = ((z * 2 + y) * 2 + k) * self.rows + cut
                    outs[step][to] = grad[pl.ds(pl.multiple_of(upper, 8), cut), :].astype(BF)
                    outs[2 + step][to] = grad[pl.ds(pl.multiple_of(lower, 8), cut), :].astype(BF)

    def send_plane(self, packed):
        return [packed[0], self.move(packed[1], 0, 0, 1), packed[2], self.move(packed[3], 0, 1, 0)]

    def plane_second(self, chunks, need=()):
        cut, depth = self.cut, self.depth
        flat = [part for held in chunks for part in held]

        def kernel(place, *refs):
            a_keep, a_out, b_keep, b_out = refs[len(flat) :]
            column = 0
            for k in range(0, len(flat), 4):
                a, a_got, b, b_got = refs[k : k + 4]
                columns = slice(column, column + a.shape[1])
                column += a.shape[1]
                for z in range(depth):
                    to = slice(z * cut, (z + 1) * cut)
                    for step in range(2):
                        y = 2 * z + lax.rem(place[1] + step, 2)
                        x = 2 * z + lax.rem(place[2] + step, 2)
                        upper = self.block(a, y, cut).astype(F32) + self.block(a_got, y, cut).astype(F32)
                        lower = self.block(b, x, cut).astype(F32) + self.block(b_got, x, cut).astype(F32)
                        if step == 0:
                            a_keep[to, columns], b_keep[to, columns] = upper, lower
                        else:
                            a_out[to, columns], b_out[to, columns] = upper.astype(BF), lower.astype(BF)

        cols = sum(held[0].shape[1] for held in chunks)
        outs = [((depth * cut, cols), kind) for kind in (F32, BF, F32, BF)]
        return self.chain.run(kernel, [(SMEM, self.place)] + [(VMEM, part) for part in flat], outs, need=need)

    def send_second(self, packed):
        return [packed[0], self.move(packed[1], 0, 1, 0), packed[2], self.move(packed[3], 0, 0, 1)]

    def plane_third(self, held):
        cut, depth = self.cut, self.depth

        def kernel(place, a, a_got, b, b_got, keep, *outs):
            for step in range(depth):
                z = lax.rem(place[0] + step, depth)
                upper = self.block(a, z, cut) + self.block(a_got, z, cut).astype(F32)
                lower = self.block(b, z, cut) + self.block(b_got, z, cut).astype(F32)
                if step == 0:
                    keep[:cut], keep[cut:] = upper, lower
                else:
                    outs[step - 1][:cut], outs[step - 1][cut:] = upper.astype(BF), lower.astype(BF)

        cols = held[0].shape[1]
        outs = [((self.rows, cols), kind) for kind in [F32] + [BF] * (depth - 1)]
        return self.chain.run(kernel, [(SMEM, self.place)] + [(VMEM, part) for part in held], outs)

    def plane_last(self, held):
        cut, depth, rows = self.cut, self.depth, self.rows

        def kernel(place, a, a_got, b, b_got, keep, out):
            for step in range(depth):
                z = lax.rem(place[0] + step, depth)
                upper = self.block(a, z, cut) + self.block(a_got, z, cut).astype(F32)
                lower = self.block(b, z, cut) + self.block(b_got, z, cut).astype(F32)
                if step == 0:
                    keep[:cut], keep[cut:] = upper, lower
                    upper, lower = jnp.zeros_like(upper), jnp.zeros_like(lower)
                out[pl.ds(pl.multiple_of(z * rows, 16), cut), :] = upper.astype(BF)
                out[pl.ds(pl.multiple_of(z * rows + cut, 16), rows - cut), :] = lower.astype(BF)

        cols = held[0].shape[1]
        outs = [((rows, cols), F32), ((depth * rows, cols), BF)]
        return self.chain.run(kernel, [(SMEM, self.place)] + [(VMEM, part) for part in held], outs)

    def send_deep(self, packed):
        return [packed[0]] + [self.move(part, j + 1) for j, part in enumerate(packed[1:])]

    def finish(self, chunks, momentum, terms):
        flat = [part for parts in chunks for part in parts]
        width = momentum.shape[1]
        each = width // 4

        def kernel(*refs):
            sources, (momentum_ref, terms_ref, moment, update, gram) = refs[: len(flat)], refs[len(flat) :]
            at = column = 0
            for parts in chunks:
                total = sources[at][...]
                for part in sources[at + 1 : at + len(parts)]:
                    for row in range(0, part.shape[0], self.rows):
                        total = total + part[row : row + self.rows].astype(F32)
                at += len(parts)
                columns = slice(column, column + total.shape[1])
                column += total.shape[1]
                value = 0.5 * momentum_ref[:, columns] + total
                moment[:, columns] = value
                update[:, columns] = total + 0.5 * value
            gram_into(4, update[...], terms_ref[...], gram)

        outs = [(momentum.shape, F32)] * 2 + [((4, each + 8, width // 2), F32)]
        operands = [(VMEM, part) for part in flat] + [(VMEM, momentum), (VMEM, terms)]
        return self.chain.run(kernel, operands, outs)


    PLANES = ((0, 1), (1, 0), (1, 1))

    def gram_first(self, parts):
        each, half = parts.shape[1:]

        def kernel(place, parts_ref, *outs):
            for (y, x), out in zip(((0, 0),) + self.PLANES, outs):
                at = lax.rem(place[1] + y, 2) * 2 + lax.rem(place[2] + x, 2)
                out[...] = parts_ref[at]

        packed = self.chain.run(kernel, [(SMEM, self.place), (VMEM, parts)], [((each, half), F32)] * 4)
        return [packed[0]] + [self.move(part, 0, *at) for part, at in zip(packed[1:], self.PLANES)]

    def add(self, parts):
        def kernel(*refs):
            total = refs[0][...]
            for part in refs[1:-1]:
                total = total + part[...]
            refs[-1][...] = total

        return self.chain.run(kernel, [(VMEM, part) for part in parts], [(parts[0].shape, F32)])[0]

    def gram_second(self, got):
        own = self.add(got)
        return [own] + self.deep(own)

    def gram_third(self, got):
        own = self.add(got)
        return [own] + [self.move(own, 0, *at) for at in self.PLANES]

    def order(self, place, j):
        return lax.rem(place[1] + j // 2, 2) * 2 + lax.rem(place[2] + j % 2, 2)


def on_box(
    n_dp,
    frames,
    cotangent,
    clip_counts,
    conv4_weight,
    conv5_weight,
    biases,
    conv4_momentum,
    conv5_momentum,
    bias_momentum,
):
    count, side, width = (frames.shape[0], frames.shape[1], frames.shape[3])
    half = width // 2
    rows = conv4_weight.shape[0]
    chain = Chain()
    box = Box(chain, n_dp, rows)
    place = box.place
    field = Field(side, count)
    low4 = conv4_weight.astype(BF)
    low5 = conv5_weight.astype(BF)
    lane = jnp.arange(width, dtype=jnp.int32) // biases.shape[0]
    own = jnp.tile(biases.astype(BF).T, (1, n_dp))
    extra = jnp.where(lane == lax.axis_index("dp"), own, jnp.zeros_like(own))
    extra = jnp.concatenate([extra, jnp.zeros((BIAS_ROWS - 2, width), BF)], axis=0)
    block4 = jnp.concatenate([low4, extra], axis=0)
    deep4 = box.deep(block4)
    pair_in = field.pair(field.flat(frames))
    mask = (jnp.arange(count, dtype=jnp.int32) < jnp.sum(clip_counts)).astype(BF)
    upstream = field.flat(cotangent * mask[:, None, None, None])
    upstream_a, upstream_b = upstream[:, :half], upstream[:, half:]
    upper4, lower4 = box.near([block4] + deep4, [*pair_in, upstream_a, upstream_b])
    x_upper4, y_lower4 = box.move(upper4, 0, 0, 1), box.move(lower4, 0, 1, 0)
    copies5, upper4 = together(jnp.concatenate([low5] * box.depth, axis=0), upper4)
    all4 = box.gather_planes(upper4, lower4, x_upper4, y_lower4)
    upper5a, lower5a, upper5b, lower5b = box.split(box.swap_deep(copies5), 2)
    x_upper5a, y_lower5a = box.move(upper5a, 0, 0, 1), box.move(lower5a, 0, 1, 0)
    x_upper5b, y_lower5b = box.move(upper5b, 0, 0, 1), box.move(lower5b, 0, 1, 0)
    box.gate([all4[0][2][1], all4[1][2][1]])
    all5a = box.gather_planes(upper5a, lower5a, x_upper5a, y_lower5a)

    tall = lower4.shape[0] // box.depth
    bias_rows = [
        (array, first + z * tall + rows - box.cut) for _, array, first in all4[1] for z in range(box.depth)
    ]
    weights4 = Weights(n_dp * rows).add(width, box.found(*all4))
    *pair_mid, slope_mid, bias = first_layer(chain, field, place, weights4, pair_in, bias_rows)
    all5b = box.gather_planes(
        upper5b, lower5b, x_upper5b, y_lower5b, [all5a[0][2][1], all5a[1][2][1]]
    )
    found5a, found5b = box.found(*all5a, fixed=True), box.found(*all5b, fixed=True)
    pack, packed = box.pack_plane, box.packed_plane(half)

    weights5a = Weights(n_dp * rows).add(half, found5a)
    layer = second_layer(
        chain, field, place, weights5a, pair_mid, bias[1:2, :half], upstream_a, pack, packed
    )
    out5a, pair5a, sum5a, packed5a = layer[0], layer[1:3], layer[3], layer[4:]
    held5a = box.send_plane(packed5a)
    weights5b = Weights(n_dp * rows).add(half, found5b)
    layer = second_layer(
        chain, field, place, weights5b, pair_mid, bias[1:2, half:], upstream_b, pack, packed
    )
    out5b, pair5b, sum5b, packed5b = layer[0], layer[1:3], layer[3], layer[4:]
    held5b = box.send_plane(packed5b)
    weights5 = Weights(n_dp * rows).add(half, found5a).add(half, found5b)
    *pair4, sum4 = back_layer(chain, field, place, weights5, [pair5a, pair5b], slope_mid)
    held5 = box.send_second(box.plane_second([held5a, held5b]))
    packed4a = weight_gradient(chain, field, place, pair_in, pair4[0], 0, half, pack, packed)
    held4a = box.send_plane(packed4a)
    packed4b = weight_gradient(chain, field, place, pair_in, pair4[0], half, half, pack, packed)
    held4b = box.send_plane(packed4b)
    kept5, out = box.plane_last(held5)
    held5 = [kept5, box.swap_deep(out)]
    input_grad = input_layer(chain, field, place, weights4, pair4)
    held4a = box.send_second(box.plane_second([held4a]))
    held4b = box.send_second(box.plane_second([held4b]))
    terms = jnp.concatenate([sum4[:, :half], sum4[:, half:], sum5a, sum5b], axis=0)
    moment5, update5, gram5 = box.finish([held5], conv5_momentum, terms)
    sums5 = box.gram_first(gram5)
    held4a = box.send_deep(box.plane_third(held4a))
    held4b = box.send_deep(box.plane_third(held4b))
    sums5 = box.gram_second(sums5)
    moment4, update4, gram4 = box.finish([held4a, held4b], conv4_momentum, jnp.zeros_like(terms))
    sums4 = box.gram_first(gram4)
    sums5 = box.gram_third(sums5)
    sums4 = box.gram_second(sums4)
    state5 = newton_first(chain, place, box.order, sums5, update5, 2)
    sums4 = box.gram_third(sums4)
    state5 = newton_next(chain, state5, 2, 4)
    new5, copy5 = newton_last(chain, state5, 4, conv5_weight)
    new4, copy4 = newton(chain, place, box.order, sums4, update4, conv4_weight)

    terms = jnp.stack([part[-8] for part in sums5]).reshape(2, 2, half)
    terms = jnp.roll(terms, (place[1], place[2]), axis=(0, 1)).reshape(2, width).T
    grad_bias = lax.dynamic_slice_in_dim(terms, lax.axis_index("dp") * biases.shape[0], biases.shape[0], 0)
    bias_moment = 0.5 * bias_momentum + grad_bias
    bias_new = biases - 0.001 * (grad_bias + 0.5 * bias_moment)
    return (
        field.unflat(jnp.concatenate([out5a, out5b], axis=1)),
        field.unflat(input_grad),
        moment4,
        moment5,
        new4,
        new5,
        copy4,
        copy5,
        bias_moment,
        bias_new,
    )


def on_device(
    frames,
    cotangent,
    clip_counts,
    conv4_weight,
    conv5_weight,
    biases,
    conv4_momentum,
    conv5_momentum,
    bias_momentum,
):
    count, side, width = (frames.shape[0], frames.shape[1], frames.shape[3])
    half = width // 2
    field = Field(side, count)
    place = jnp.zeros((3,), jnp.int32)
    chain = Chain()

    def gather(value):
        return lax.all_gather(value.astype(BF), "dp", axis=0, tiled=True)

    def scatter(value):
        return lax.psum_scatter(value, "dp", scatter_dimension=0, tiled=True)

    def weights(*arrays):
        total = arrays[0].shape[0]
        result = Weights(total)
        for array in arrays:
            result.add(array.shape[1], [(array, 0, 0, total, lambda place: 0)])
        return result

    def keep(place_ref, grad, outs):
        outs[0][...] = grad[...]

    full4, full5 = gather(conv4_weight), gather(conv5_weight)
    bias_block = jnp.pad(gather(biases).T, ((0, BIAS_ROWS - 2), (0, 0)))
    pair_in = field.pair(field.flat(frames))
    mask = (jnp.arange(count, dtype=jnp.int32) < jnp.sum(clip_counts)).astype(BF)
    upstream = field.flat(cotangent * mask[:, None, None, None])
    whole = [((full4.shape[0], half), F32)]
    weights4 = weights(full4)
    weights4.arrays.append(bias_block)
    *pair_mid, slope_mid, bias = first_layer(chain, field, place, weights4, pair_in, [(bias_block, 0)])
    parts = []
    for columns in (slice(0, half), slice(half, width)):
        parts.append(
            second_layer(
                chain, field, place, weights(full5[:, columns]), pair_mid, bias[1:2, columns], upstream[:, columns], keep, whole
            )
        )
    back = [part[1:3] for part in parts]
    *pair4, sum4 = back_layer(chain, field, place, weights(full5[:, :half], full5[:, half:]), back, slope_mid)
    grad5 = scatter(jnp.concatenate([part[4] for part in parts], axis=1))
    grad4 = scatter(
        jnp.concatenate(
            [weight_gradient(chain, field, place, pair_in, pair4[0], at, half, keep, whole)[0] for at in (0, half)], axis=1
        )
    )
    input_grad = input_layer(chain, field, place, weights(full4), pair4)
    grad_bias = scatter(jnp.concatenate([sum4, parts[0][3], parts[1][3]], axis=1).reshape(2, width).T)

    def step(grad, momentum, weight):
        moment = 0.5 * momentum + grad
        update = grad + 0.5 * moment

        def kernel(update_ref, gram_ref):
            gram_into(4, update_ref[...], jnp.zeros((4, half), F32), gram_ref)

        gram = chain.run(kernel, [(VMEM, update)], [((4, width // 4 + 8, half), F32)])[0]
        gram = lax.psum(gram, "dp")
        new, copy = newton(chain, place, lambda place, j: j, [gram[k] for k in range(4)], update, weight)
        return moment, new, copy

    moment4, new4, copy4 = step(grad4, conv4_momentum, conv4_weight)
    moment5, new5, copy5 = step(grad5, conv5_momentum, conv5_weight)
    bias_moment = 0.5 * bias_momentum + grad_bias
    bias_new = biases - 0.001 * (grad_bias + 0.5 * bias_moment)
    return (
        field.unflat(jnp.concatenate([part[0] for part in parts], axis=1)),
        field.unflat(input_grad),
        moment4,
        moment5,
        new4,
        new5,
        copy4,
        copy5,
        bias_moment,
        bias_new,
    )


def solution(mesh):
    n = mesh.shape["dp"]
    rows = P(("stream", "dp"), None)
    field = P(("stream", "dp"), None, None, None)

    def program(*arrays):
        own = arrays[3].shape[0]
        if n % 4 == 0 and n > 4 and own % 32 == 0:
            return on_box(n, *arrays)
        return on_device(*arrays)

    return jax.shard_map(
        program,
        mesh=mesh,
        in_specs=(field, field, P(("stream", "dp")), rows, rows, rows, rows, rows, rows),
        out_specs=(field, field) + (rows,) * 8,
        check_vma=False,
    )
```

```python
import functools
import math

import jax
import jax.numpy as jnp
from jax import lax
from jax.experimental import pallas as pl
from jax.experimental.pallas import tpu as pltpu
from jax.sharding import PartitionSpec as P

NS_STEPS = 5
BIAS_ROWS = 16
BLOCK = 256
LANES = 128
BF = jnp.bfloat16
F32 = jnp.float32
VMEM = pl.BlockSpec(memory_space=pltpu.VMEM)
SMEM = pl.BlockSpec(memory_space=pltpu.SMEM)
ANY = pl.BlockSpec(memory_space=pl.ANY)
HBM = pl.BlockSpec(memory_space=pltpu.HBM)


def together(*values):
    return lax.optimization_barrier(values)


class Chain:
    def __init__(self):
        self.link = None

    def run(self, kernel, operands, outs, scratch=(), limit=14, need=()):
        before = list(need) + ([] if self.link is None else [self.link])
        n, m = len(operands), len(before)

        def linked(*refs):
            link = refs[n + m + len(outs)]
            kernel(*refs[:n], *refs[n + m : n + m + len(outs)], *refs[n + m + len(outs) + 1 :])
            link[...] = jnp.zeros_like(link)

        result = pl.pallas_call(
            linked,
            in_specs=[spec for spec, _ in operands] + [ANY] * m,
            out_specs=[VMEM] * (len(outs) + 1),
            out_shape=[jax.ShapeDtypeStruct(shape, kind) for shape, kind in outs + [((8, 128), F32)]],
            scratch_shapes=list(scratch),
            compiler_params=pltpu.CompilerParams(vmem_limit_bytes=limit * 1024 * 1024),
            cost_estimate=pl.CostEstimate(flops=1, bytes_accessed=100_000, transcendentals=0),
        )(*[array for _, array in operands], *before)
        *results, self.link = result
        return results


def copy_all(pairs, sem):
    copies = [pltpu.make_async_copy(source, target, sem.at[k]) for k, (source, target) in enumerate(pairs)]
    for copy in copies:
        copy.start()
    for copy in copies:
        copy.wait()


class Field:
    def __init__(self, side, count):
        self.side, self.count = side, count
        self.line = (side + 1) * count
        self.cells = side * self.line
        self.lead = -(-self.line // 16) * 16 + 16
        self.rows = -(-(self.lead + self.cells + self.line + count) // 16) * 16

    def tap(self, r, s):
        start = self.lead + (r - 1) * self.line + (s - 1) * self.count
        return (0, start) if start % 16 == 0 else (1, start - self.count)

    def flat(self, values):
        cells = jnp.transpose(values, (1, 2, 0, 3))
        cells = jnp.pad(cells, ((0, 0), (0, 1), (0, 0), (0, 0)))
        return cells.reshape(self.cells, -1)

    def pair(self, flat):
        after = self.rows - self.lead - self.cells
        return (
            jnp.pad(flat, ((self.lead, after), (0, 0))),
            jnp.pad(flat, ((self.lead - self.count, after + self.count), (0, 0))),
        )

    def unflat(self, flat):
        cells = flat.reshape(self.side, self.side + 1, self.count, -1)[:, : self.side]
        return jnp.transpose(cells, (2, 0, 1, 3))

    def sweep(self, wide, pair, columns, body):
        count, lead, line, cells = self.count, self.lead, self.line, self.cells
        width = wide.shape[1]
        pad = jnp.zeros((count, LANES), F32)

        totals = [jnp.zeros((8, LANES), F32)] * (width // LANES)
        for row in range(0, cells, line):
            for c in range(0, width, LANES):
                some = slice(columns.start + c, columns.start + c + LANES)
                value = body(slice(row, row + line), some, wide[row + count : row + count + line, c : c + LANES])
                value = jnp.concatenate([value[: line - count], pad], axis=0)
                low = value.astype(BF)
                pair[0][lead + row : lead + row + line, some] = low
                value = low.astype(F32)
                wide[row + count : row + count + line, c : c + LANES] = value
                totals[c // LANES] = totals[c // LANES] + jnp.sum(value.reshape(line // 8, 8, LANES), axis=0)
        wide[0:count] = jnp.zeros((count, width), F32)
        wide[count + cells :] = jnp.zeros((count, width), F32)
        end = self.rows - lead - cells
        pair[0][0:lead, columns] = jnp.zeros((lead, width), BF)
        pair[0][lead + cells :, columns] = jnp.zeros((end, width), BF)
        pair[1][0 : lead - 16, columns] = jnp.zeros((lead - 16, width), BF)
        pair[1][lead + cells :, columns] = jnp.zeros((end, width), BF)
        pair[1][lead - 16 : lead + cells, columns] = wide[0 : cells + 16, :].astype(BF)
        return jnp.concatenate([jnp.sum(total, axis=0, keepdims=True) for total in totals], axis=1)

    def wide(self):
        return pltpu.VMEM((self.cells + 2 * self.count, BLOCK), F32)


def convolve_block(field, pair, full, columns):
    width = pair[0].shape[1]
    total = None
    for r in range(3):
        for s in range(3):
            which, start = field.tap(r, s)
            tap = (3 * r + s) * width
            part = jnp.dot(
                pair[which][start : start + field.cells, :],
                full[tap : tap + width, columns],
                preferred_element_type=F32,
            )
            total = part if total is None else total + part
    return total


def convolve_back_block(field, pairs, full, at, cols):
    width = full.shape[0] // 9
    total = None
    for r in range(3):
        for s in range(3):
            which, start = field.tap(2 - r, 2 - s)
            tap = (3 * r + s) * width + at
            begin = 0
            for pair in pairs:
                end = begin + pair[0].shape[1]
                part = lax.dot_general(
                    pair[which][start : start + field.cells, :],
                    full[tap : tap + cols, begin:end],
                    (((1,), (1,)), ((), ())),
                    preferred_element_type=F32,
                )
                total = part if total is None else total + part
                begin = end
    return total


def gradient_into(field, pair, delta, out, looped):
    width = pair[0].shape[1]

    def line(r, carry):
        for s in range(3):
            which, start = field.tap(0, s)
            start = start + r * field.line
            tap = (3 * r + s) * width
            if looped:
                start, tap = pl.multiple_of(start, 16), pl.multiple_of(tap, width)
            out[pl.ds(tap, width), :] = lax.dot_general(
                pair[which][pl.ds(start, field.cells), :], delta[...], (((0,), (0,)), ((), ())), preferred_element_type=F32
            )
        return carry

    if looped:
        lax.fori_loop(0, 3, line, 0)
    else:
        for r in range(3):
            line(r, 0)


def activate(value):
    square = value * value
    slope = 0.7978845608
    bend = jnp.tanh(slope * value * (1.0 + 0.044715 * square))
    rise = 0.5 * (1.0 + bend)
    steep = slope * (1.0 + 3 * 0.044715 * square)
    return value * rise, rise + 0.5 * value * (1.0 - bend * bend) * steep


class Weights:
    def __init__(self, total):
        self.total, self.cols = total, 0
        self.arrays, self.plan = [], []

    def add(self, cols, found):
        for part, start, left, height, where in found:
            if not any(other is part for other in self.arrays):
                self.arrays.append(part)
            which = [k for k, other in enumerate(self.arrays) if other is part][0]
            self.plan.append((which, start, left, height, where, self.cols, cols))
        self.cols += cols
        return self

    def operands(self):
        return [(HBM, array) for array in self.arrays]

    def scratch(self, more=0):
        return [pltpu.VMEM((self.total, self.cols), BF), pltpu.SemaphoreType.DMA((len(self.plan) + more,))]

    def copies(self, place, arrays, full):
        return [
            (
                arrays[which].at[pl.ds(start, height), pl.ds(left, cols)],
                full.at[pl.ds(pl.multiple_of(where(place), 16), height), pl.ds(column, cols)],
            )
            for which, start, left, height, where, column, cols in self.plan
        ]


def first_layer(chain, field, place, weights, pair, bias_rows):
    width = weights.cols
    n = len(weights.arrays)
    sources = [([other is array for other in weights.arrays].index(True), row) for array, row in bias_rows]

    def kernel(*refs):
        place_ref, arrays, rest = refs[0], refs[1 : n + 1], refs[n + 1 :]
        even_in, odd_in, out_even, out_odd, slope_ref, bias_ref, even, odd, terms, wide, full, sem = rest
        lines = [
            (arrays[which].at[pl.ds(row, BIAS_ROWS)], terms.at[pl.ds(k * BIAS_ROWS, BIAS_ROWS)])
            for k, (which, row) in enumerate(sources)
        ]
        copy_all(weights.copies(place_ref, arrays, full) + [(even_in, even), (odd_in, odd)] + lines, sem)
        total = terms[0:BIAS_ROWS].astype(F32)
        for k in range(1, len(lines)):
            total = total + terms[k * BIAS_ROWS : (k + 1) * BIAS_ROWS].astype(F32)
        bias_ref[...] = total
        for at in range(0, width, BLOCK):
            columns = slice(at, at + BLOCK)
            wide[field.count : field.count + field.cells] = convolve_block(field, (even, odd), full, columns)

            def body(rows, some, value):
                result, slope_ref[rows, some] = activate(value + bias_ref[0:1, some])
                return result

            field.sweep(wide, (out_even, out_odd), columns, body)

    form = pltpu.VMEM(pair[0].shape, BF)
    terms = pltpu.VMEM((len(sources) * BIAS_ROWS, width), BF)
    return chain.run(
        kernel,
        [(SMEM, place)] + weights.operands() + [(HBM, pair[0]), (HBM, pair[1])],
        [((field.rows, width), BF)] * 2 + [((field.cells, width), F32), ((BIAS_ROWS, width), F32)],
        [form, form, terms, field.wide()] + weights.scratch(2 + len(sources)),
        limit=54,
    )


def second_layer(chain, field, place, weights, pair, bias, upstream, pack, packed, need=()):
    width = weights.cols
    n = len(weights.arrays)

    def kernel(*refs):
        place_ref, arrays, rest = refs[0], refs[1 : n + 1], refs[n + 1 :]
        even, odd, bias_ref, up_in, out_ref, d_even, d_odd, sum_ref, *outs, grad, up_ref, wide, full, sem = rest
        copy_all(weights.copies(place_ref, arrays, full) + [(up_in, up_ref)], sem)
        wide[field.count : field.count + field.cells] = convolve_block(field, (even, odd), full, slice(0, width))

        def body(rows, some, value):
            result, slope = activate(value + bias_ref[:, some])
            out_ref[rows, some] = result.astype(BF)
            return up_ref[rows, some].astype(F32) * slope

        sum_ref[...] = field.sweep(wide, (d_even, d_odd), slice(0, width), body)
        gradient_into(field, (even, odd), d_even.at[pl.ds(field.lead, field.cells)], grad, True)
        pack(place_ref, grad, outs)

    form = ((field.rows, width), BF)
    return chain.run(
        kernel,
        [(SMEM, place)] + weights.operands() + [(VMEM, pair[0]), (VMEM, pair[1]), (VMEM, bias), (HBM, upstream)],
        [((field.cells, width), BF), form, form, ((1, width), F32)] + packed,
        [pltpu.VMEM((9 * pair[0].shape[1], width), F32), pltpu.VMEM((field.cells, width), BF)]
        + [field.wide()]
        + weights.scratch(1),
        limit=24,
        need=need,
    )


def back_layer(chain, field, place, weights, pairs, slope, need=()):
    width = weights.total // 9
    n = len(weights.arrays)
    flat = [form for pair in pairs for form in pair]

    def kernel(*refs):
        place_ref, arrays, rest = refs[0], refs[1 : n + 1], refs[n + 1 :]
        deltas, rest = rest[: len(flat)], rest[len(flat) :]
        slope_in, d_even, d_odd, sum_ref, slope_ref, wide, full, sem = rest
        copy_all(weights.copies(place_ref, arrays, full) + [(slope_in, slope_ref)], sem)
        held = [deltas[k : k + 2] for k in range(0, len(flat), 2)]
        for at in range(0, width, BLOCK):
            columns = slice(at, at + BLOCK)
            wide[field.count : field.count + field.cells] = convolve_back_block(field, held, full, at, BLOCK)

            def body(rows, some, value):
                return value * slope_ref[rows, some]

            sum_ref[:, columns] = field.sweep(wide, (d_even, d_odd), columns, body)

    return chain.run(
        kernel,
        [(SMEM, place)] + weights.operands() + [(VMEM, form) for form in flat] + [(HBM, slope)],
        [((field.rows, width), BF)] * 2 + [((1, width), F32)],
        [pltpu.VMEM(slope.shape, F32), field.wide()]
        + weights.scratch(1),
        limit=24,
        need=need,
    )


def input_layer(chain, field, place, weights, pair):
    n = len(weights.arrays)
    width = weights.total // 9

    def kernel(*refs):
        place_ref, arrays, rest = refs[0], refs[1 : n + 1], refs[n + 1 :]
        even_in, odd_in, out_ref, even, odd, full, sem = rest
        copy_all(weights.copies(place_ref, arrays, full) + [(even_in, even), (odd_in, odd)], sem)
        for at in range(0, width, BLOCK):
            out_ref[:, at : at + BLOCK] = convolve_back_block(field, [(even, odd)], full, at, BLOCK).astype(BF)

    operands = [(SMEM, place)] + weights.operands() + [(ANY, pair[0]), (ANY, pair[1])]
    form = pltpu.VMEM(pair[0].shape, BF)
    return chain.run(kernel, operands, [((field.cells, width), BF)], [form, form] + weights.scratch(2), limit=54)[0]


def weight_gradient(chain, field, place, pair, delta, at, cols, pack, packed, need=()):
    width = pair[0].shape[1]

    def kernel(place_ref, even_in, odd_in, delta_ref, *rest):
        *outs, even, odd, grad, sem = rest
        copy_all([(even_in, even), (odd_in, odd)], sem)
        delta = delta_ref.at[pl.ds(field.lead, field.cells), pl.ds(at, cols)]
        gradient_into(field, (even, odd), delta, grad, False)
        pack(place_ref, grad, outs)

    form = pltpu.VMEM(pair[0].shape, BF)
    return chain.run(
        kernel,
        [(SMEM, place), (HBM, pair[0]), (HBM, pair[1]), (VMEM, delta)],
        packed,
        [form, form, pltpu.VMEM((9 * width, cols), F32), pltpu.SemaphoreType.DMA((2,))],
        limit=20,
        need=need,
    )


def halves(value):
    high = value.astype(BF)
    return high, (value - high.astype(F32)).astype(BF)


def product(left, right):
    return jnp.dot(
        jnp.concatenate([left[0], left[0], left[1]], axis=1),
        jnp.concatenate([right[0], right[1], right[0]], axis=0),
        preferred_element_type=F32,
    )


def square_masks(size):
    row = lax.broadcasted_iota(jnp.int32, (size, size), 0)
    column = lax.broadcasted_iota(jnp.int32, (size, size), 1)
    return row, column


def gram_into(parts, update, terms, out_ref):
    low = update.astype(BF)
    half = low.shape[1] // 2
    each = 2 * half // parts
    left, right = low[:, :half], low[:, half:]

    def block(one, two):
        return lax.dot_general(one, two, (((0,), (0,)), ((), ())), preferred_element_type=F32)

    row, column = square_masks(half)
    last = block(right, right)
    for k, value in enumerate((block(left, right), jnp.where(column >= row, block(left, left), last))):
        for part in range(parts):
            first = max(part * each, k * half)
            end = min((part + 1) * each, (k + 1) * half)
            if first < end:
                out_ref[part, first - part * each : end - part * each] = value[first - k * half : end - k * half]
    diagonal = jnp.sum(jnp.where(column == row, last, 0.0), axis=0, keepdims=True)
    for part in range(parts):
        out_ref[part, each : each + 1] = terms[part : part + 1]
        out_ref[part, each + 1 : each + 2] = diagonal if part == 0 else jnp.zeros_like(diagonal)
        out_ref[part, each + 2 :] = jnp.zeros((6, half), F32)


def newton_start(order, place_ref, sums, update_ref, packed, below):
    each = packed.shape[0] // len(sums)
    for j, part in enumerate(sums):
        at = order(place_ref, j)
        packed[pl.ds(pl.multiple_of(at * each, 8), each), :] = part[:each]
        below[pl.ds(pl.multiple_of(at * 8, 8), 8), :] = part[each:]
    half = packed.shape[1]
    row, column = square_masks(half)
    corner = packed[:half]
    mixed = packed[half:]
    turned = mixed.T
    last = jnp.where(column < row, mixed, jnp.where(column > row, turned, below[1:2]))
    gram = jnp.concatenate(
        [
            jnp.concatenate([jnp.where(column >= row, mixed, turned), corner], axis=1),
            jnp.concatenate([corner.T, last], axis=1),
        ],
        axis=0,
    )
    square = jnp.sum(jnp.where(column == row, mixed, 0.0)) + jnp.sum(below[1:2])
    scale = 1.0 / (jnp.sqrt(square) + 1e-07)
    return gram * scale * scale, update_ref[...] * scale


def newton_steps(gram, iterate, steps):
    for step in steps:
        parts = halves(gram)
        poly = halves(-4.775 * gram + 2.0315 * product(parts, parts))
        iterate = 3.4445 * iterate + product(halves(iterate), poly)
        if step < NS_STEPS - 1:
            middle = 3.4445 * gram + product(parts, poly)
            gram = 3.4445 * middle + product(halves(middle), poly)
    return gram, iterate


def newton(chain, place, order, sums, update, weight):
    width = weight.shape[1]
    n = len(sums)

    def kernel(place_ref, *refs):
        update_ref, weight_ref, new_ref, copy_ref, packed, below = refs[n:]
        state = newton_start(order, place_ref, refs[:n], update_ref, packed, below)
        new = weight_ref[...] - newton_steps(*state, range(NS_STEPS))[1]
        new_ref[...] = new
        copy_ref[...] = new.astype(BF)

    return chain.run(
        kernel,
        [(SMEM, place)] + [(VMEM, part) for part in sums] + [(VMEM, update), (VMEM, weight)],
        [(weight.shape, F32), (weight.shape, BF)],
        [pltpu.VMEM((width, width // 2), F32), pltpu.VMEM((8 * n, width // 2), F32)],
    )


def newton_first(chain, place, order, sums, update, last):
    width = update.shape[1]
    n = len(sums)

    def kernel(place_ref, *refs):
        update_ref, gram_ref, iterate_ref, packed, below = refs[n:]
        state = newton_start(order, place_ref, refs[:n], update_ref, packed, below)
        gram_ref[...], iterate_ref[...] = newton_steps(*state, range(last))

    return chain.run(
        kernel,
        [(SMEM, place)] + [(VMEM, part) for part in sums] + [(VMEM, update)],
        [((width, width), F32), (update.shape, F32)],
        [pltpu.VMEM((width, width // 2), F32), pltpu.VMEM((8 * n, width // 2), F32)],
    )


def newton_next(chain, state, first, last):
    def kernel(gram_ref, iterate_ref, gram_out, iterate_out):
        gram_out[...], iterate_out[...] = newton_steps(gram_ref[...], iterate_ref[...], range(first, last))

    return chain.run(kernel, [(VMEM, part) for part in state], [(part.shape, F32) for part in state])


def newton_last(chain, state, first, weight):
    def kernel(gram_ref, iterate_ref, weight_ref, new_ref, copy_ref):
        new = weight_ref[...] - newton_steps(gram_ref[...], iterate_ref[...], range(first, NS_STEPS))[1]
        new_ref[...] = new
        copy_ref[...] = new.astype(BF)

    operands = [(VMEM, part) for part in state] + [(VMEM, weight)]
    return chain.run(kernel, operands, [(weight.shape, F32), (weight.shape, BF)])


class Box:
    def __init__(self, chain, n, rows):
        self.chain = chain
        self.depth = n // 4
        self.n, self.rows, self.cut = n, rows, rows // 2
        me = lax.axis_index("dp")
        self.place = jnp.stack([me // 4, me // 2 % 2, me % 2]).astype(jnp.int32)

    def move(self, block, z, y=0, x=0):
        pairs = []
        for index in range(self.n):
            to = ((index // 4 + z) % self.depth) * 4 + ((index // 2 + y) % 2) * 2 + (index + x) % 2
            pairs.append((index, to))
        return lax.ppermute(block, "dp", pairs)

    def deep(self, block):
        return [self.move(block, -j) for j in range(1, self.depth)]

    def swap_deep(self, blocks):
        groups = [[4 * z + k for z in range(self.depth)] for k in range(4)]
        return lax.all_to_all(blocks, "dp", 0, 0, axis_index_groups=groups, tiled=True)

    def owner(self, z, y, x, fixed):
        def where(place):
            at = z if fixed else lax.rem(place[0] + z, self.depth)
            return ((at * 2 + lax.rem(place[1] + y, 2)) * 2 + lax.rem(place[2] + x, 2)) * self.rows

        return where


    def split(self, blocks, parts):
        cut, low = self.cut, blocks[0].shape[0] - self.cut
        cols = blocks[0].shape[1] // parts

        def kernel(*refs):
            sources, outs = refs[: len(blocks)], refs[len(blocks) :]
            for k in range(parts):
                columns = slice(k * cols, (k + 1) * cols)
                for j, source in enumerate(sources):
                    outs[2 * k][j * cut : (j + 1) * cut] = source[:cut, columns]
                    outs[2 * k + 1][j * low : (j + 1) * low] = source[cut:, columns]

        outs = [((len(blocks) * cut, cols), BF), ((len(blocks) * low, cols), BF)] * parts
        return self.chain.run(kernel, [(VMEM, block) for block in blocks], outs)

    def gate(self, arrays):
        def kernel(out):
            out[...] = jnp.zeros_like(out)

        self.chain.run(kernel, [], [((8, 128), F32)], need=arrays)

    def near(self, blocks, need=()):
        cut, tall = self.cut, blocks[0].shape[0]
        low = tall - cut

        def kernel(*refs):
            *sources, upper, lower = refs
            for j, source in enumerate(sources):
                upper[j * cut : (j + 1) * cut] = source[:cut]
                lower[j * low : (j + 1) * low] = source[cut:]

        cols = blocks[0].shape[1]
        outs = [((len(blocks) * cut, cols), BF), ((len(blocks) * low, cols), BF)]
        return self.chain.run(kernel, [(VMEM, block) for block in blocks], outs, need=need)

    def found(self, upper, lower, tall, fixed=False):
        pieces = []
        for at, height, arrays in ((0, tall[0], upper), (self.cut, tall[1], lower)):
            for (y, x), array, first in arrays:
                for z in range(self.depth):
                    where = functools.partial(lambda f, a, p: f(p) + a, self.owner(z, y, x, fixed), at)
                    pieces.append((array, first + z * height // self.depth, 0, self.cut, where))
        return pieces

    def gather_planes(self, upper, lower, x_upper, y_lower, need=()):
        tall = upper.shape[0], lower.shape[0]
        cols = upper.shape[1]

        def kernel(a, a_got, b, b_got, a_wide, b_wide):
            a_wide[: tall[0]], a_wide[tall[0] :] = a[...], a_got[...]
            b_wide[: tall[1]], b_wide[tall[1] :] = b[...], b_got[...]

        operands = [(VMEM, array) for array in (upper, x_upper, lower, y_lower)]
        wide = self.chain.run(kernel, operands, [((2 * height, cols), BF) for height in tall], need=need)
        y_wide, x_wide = self.move(wide[0], 0, 1, 0), self.move(wide[1], 0, 0, 1)
        uppers = [((0, 0), wide[0], 0), ((0, 1), wide[0], tall[0]), ((1, 0), y_wide, 0), ((1, 1), y_wide, tall[0])]
        lowers = [((0, 0), wide[1], 0), ((1, 0), wide[1], tall[1]), ((0, 1), x_wide, 0), ((1, 1), x_wide, tall[1])]
        return uppers, lowers, tall


    def block(self, ref, index, rows):
        return ref[pl.ds(pl.multiple_of(index * rows, 8), rows), :]

    def packed_plane(self, cols):
        tall = 2 * self.depth * self.cut
        return [((tall, cols), BF)] * 4

    def pack_plane(self, place, grad, outs):
        cut = self.cut
        for z in range(self.depth):
            for k in range(2):
                to = slice((2 * z + k) * cut, (2 * z + k + 1) * cut)
                for step in range(2):
                    x = lax.rem(place[2] + step, 2)
                    y = lax.rem(place[1] + step, 2)
                    upper = ((z * 2 + k) * 2 + x) * self.rows
                    lower = ((z * 2 + y) * 2 + k) * self.rows + cut
                    outs[step][to] = grad[pl.ds(pl.multiple_of(upper, 8), cut), :].astype(BF)
                    outs[2 + step][to] = grad[pl.ds(pl.multiple_of(lower, 8), cut), :].astype(BF)

    def send_plane(self, packed):
        return [packed[0], self.move(packed[1], 0, 0, 1), packed[2], self.move(packed[3], 0, 1, 0)]

    def plane_second(self, chunks, need=()):
        cut, depth = self.cut, self.depth
        flat = [part for held in chunks for part in held]

        def kernel(place, *refs):
            a_keep, a_out, b_keep, b_out = refs[len(flat) :]
            column = 0
            for k in range(0, len(flat), 4):
                a, a_got, b, b_got = refs[k : k + 4]
                columns = slice(column, column + a.shape[1])
                column += a.shape[1]
                for z in range(depth):
                    to = slice(z * cut, (z + 1) * cut)
                    for step in range(2):
                        y = 2 * z + lax.rem(place[1] + step, 2)
                        x = 2 * z + lax.rem(place[2] + step, 2)
                        upper = self.block(a, y, cut).astype(F32) + self.block(a_got, y, cut).astype(F32)
                        lower = self.block(b, x, cut).astype(F32) + self.block(b_got, x, cut).astype(F32)
                        if step == 0:
                            a_keep[to, columns], b_keep[to, columns] = upper, lower
                        else:
                            a_out[to, columns], b_out[to, columns] = upper.astype(BF), lower.astype(BF)

        cols = sum(held[0].shape[1] for held in chunks)
        outs = [((depth * cut, cols), kind) for kind in (F32, BF, F32, BF)]
        return self.chain.run(kernel, [(SMEM, self.place)] + [(VMEM, part) for part in flat], outs, need=need)

    def send_second(self, packed):
        return [packed[0], self.move(packed[1], 0, 1, 0), packed[2], self.move(packed[3], 0, 0, 1)]

    def plane_third(self, held):
        cut, depth = self.cut, self.depth

        def kernel(place, a, a_got, b, b_got, keep, *outs):
            for step in range(depth):
                z = lax.rem(place[0] + step, depth)
                upper = self.block(a, z, cut) + self.block(a_got, z, cut).astype(F32)
                lower = self.block(b, z, cut) + self.block(b_got, z, cut).astype(F32)
                if step == 0:
                    keep[:cut], keep[cut:] = upper, lower
                else:
                    outs[step - 1][:cut], outs[step - 1][cut:] = upper.astype(BF), lower.astype(BF)

        cols = held[0].shape[1]
        outs = [((self.rows, cols), kind) for kind in [F32] + [BF] * (depth - 1)]
        return self.chain.run(kernel, [(SMEM, self.place)] + [(VMEM, part) for part in held], outs)

    def plane_last(self, held):
        cut, depth, rows = self.cut, self.depth, self.rows

        def kernel(place, a, a_got, b, b_got, keep, out):
            for step in range(depth):
                z = lax.rem(place[0] + step, depth)
                upper = self.block(a, z, cut) + self.block(a_got, z, cut).astype(F32)
                lower = self.block(b, z, cut) + self.block(b_got, z, cut).astype(F32)
                if step == 0:
                    keep[:cut], keep[cut:] = upper, lower
                    upper, lower = jnp.zeros_like(upper), jnp.zeros_like(lower)
                out[pl.ds(pl.multiple_of(z * rows, 16), cut), :] = upper.astype(BF)
                out[pl.ds(pl.multiple_of(z * rows + cut, 16), rows - cut), :] = lower.astype(BF)

        cols = held[0].shape[1]
        outs = [((rows, cols), F32), ((depth * rows, cols), BF)]
        return self.chain.run(kernel, [(SMEM, self.place)] + [(VMEM, part) for part in held], outs)

    def send_deep(self, packed):
        return [packed[0]] + [self.move(part, j + 1) for j, part in enumerate(packed[1:])]

    def finish(self, chunks, momentum, terms):
        flat = [part for parts in chunks for part in parts]
        width = momentum.shape[1]
        each = width // 4

        def kernel(*refs):
            sources, (momentum_ref, terms_ref, moment, update, gram) = refs[: len(flat)], refs[len(flat) :]
            at = column = 0
            for parts in chunks:
                total = sources[at][...]
                for part in sources[at + 1 : at + len(parts)]:
                    for row in range(0, part.shape[0], self.rows):
                        total = total + part[row : row + self.rows].astype(F32)
                at += len(parts)
                columns = slice(column, column + total.shape[1])
                column += total.shape[1]
                value = 0.5 * momentum_ref[:, columns] + total
                moment[:, columns] = value
                update[:, columns] = total + 0.5 * value
            gram_into(4, update[...], terms_ref[...], gram)

        outs = [(momentum.shape, F32)] * 2 + [((4, each + 8, width // 2), F32)]
        operands = [(VMEM, part) for part in flat] + [(VMEM, momentum), (VMEM, terms)]
        return self.chain.run(kernel, operands, outs)


    PLANES = ((0, 1), (1, 0), (1, 1))

    def gram_first(self, parts):
        each, half = parts.shape[1:]

        def kernel(place, parts_ref, *outs):
            for (y, x), out in zip(((0, 0),) + self.PLANES, outs):
                at = lax.rem(place[1] + y, 2) * 2 + lax.rem(place[2] + x, 2)
                out[...] = parts_ref[at]

        packed = self.chain.run(kernel, [(SMEM, self.place), (VMEM, parts)], [((each, half), F32)] * 4)
        return [packed[0]] + [self.move(part, 0, *at) for part, at in zip(packed[1:], self.PLANES)]

    def add(self, parts):
        def kernel(*refs):
            total = refs[0][...]
            for part in refs[1:-1]:
                total = total + part[...]
            refs[-1][...] = total

        return self.chain.run(kernel, [(VMEM, part) for part in parts], [(parts[0].shape, F32)])[0]

    def gram_second(self, got):
        own = self.add(got)
        return [own] + self.deep(own)

    def gram_third(self, got):
        own = self.add(got)
        return [own] + [self.move(own, 0, *at) for at in self.PLANES]

    def order(self, place, j):
        return lax.rem(place[1] + j // 2, 2) * 2 + lax.rem(place[2] + j % 2, 2)


def on_box(
    n_dp,
    frames,
    cotangent,
    clip_counts,
    conv4_weight,
    conv5_weight,
    biases,
    conv4_momentum,
    conv5_momentum,
    bias_momentum,
):
    count, side, width = (frames.shape[0], frames.shape[1], frames.shape[3])
    half = width // 2
    rows = conv4_weight.shape[0]
    chain = Chain()
    box = Box(chain, n_dp, rows)
    place = box.place
    field = Field(side, count)
    low4 = conv4_weight.astype(BF)
    low5 = conv5_weight.astype(BF)
    lane = jnp.arange(width, dtype=jnp.int32) // biases.shape[0]
    own = jnp.tile(biases.astype(BF).T, (1, n_dp))
    extra = jnp.where(lane == lax.axis_index("dp"), own, jnp.zeros_like(own))
    extra = jnp.concatenate([extra, jnp.zeros((BIAS_ROWS - 2, width), BF)], axis=0)
    block4 = jnp.concatenate([low4, extra], axis=0)
    deep4 = box.deep(block4)
    pair_in = field.pair(field.flat(frames))
    mask = (jnp.arange(count, dtype=jnp.int32) < jnp.sum(clip_counts)).astype(BF)
    upstream = field.flat(cotangent * mask[:, None, None, None])
    upstream_a, upstream_b = upstream[:, :half], upstream[:, half:]
    upper4, lower4 = box.near([block4] + deep4, [*pair_in, upstream_a, upstream_b])
    x_upper4, y_lower4 = box.move(upper4, 0, 0, 1), box.move(lower4, 0, 1, 0)
    all4 = box.gather_planes(upper4, lower4, x_upper4, y_lower4)
    upper5a, lower5a, upper5b, lower5b = box.split([low5] + box.deep(low5), 2)
    x_upper5a, y_lower5a = box.move(upper5a, 0, 0, 1), box.move(lower5a, 0, 1, 0)
    x_upper5b, y_lower5b = box.move(upper5b, 0, 0, 1), box.move(lower5b, 0, 1, 0)
    box.gate([all4[0][2][1], all4[1][2][1]])
    all5a = box.gather_planes(upper5a, lower5a, x_upper5a, y_lower5a)

    tall = lower4.shape[0] // box.depth
    bias_rows = [
        (array, first + z * tall + rows - box.cut) for _, array, first in all4[1] for z in range(box.depth)
    ]
    weights4 = Weights(n_dp * rows).add(width, box.found(*all4))
    *pair_mid, slope_mid, bias = first_layer(chain, field, place, weights4, pair_in, bias_rows)
    all5b = box.gather_planes(
        upper5b, lower5b, x_upper5b, y_lower5b, [all5a[0][2][1], all5a[1][2][1]]
    )
    found5a, found5b = box.found(*all5a), box.found(*all5b)
    pack, packed = box.pack_plane, box.packed_plane(half)

    weights5a = Weights(n_dp * rows).add(half, found5a)
    layer = second_layer(
        chain, field, place, weights5a, pair_mid, bias[1:2, :half], upstream_a, pack, packed
    )
    out5a, pair5a, sum5a, packed5a = layer[0], layer[1:3], layer[3], layer[4:]
    held5a = box.send_plane(packed5a)
    weights5b = Weights(n_dp * rows).add(half, found5b)
    layer = second_layer(
        chain, field, place, weights5b, pair_mid, bias[1:2, half:], upstream_b, pack, packed
    )
    out5b, pair5b, sum5b, packed5b = layer[0], layer[1:3], layer[3], layer[4:]
    held5b = box.send_plane(packed5b)
    weights5 = Weights(n_dp * rows).add(half, found5a).add(half, found5b)
    *pair4, sum4 = back_layer(chain, field, place, weights5, [pair5a, pair5b], slope_mid)
    held5 = box.send_second(box.plane_second([held5a, held5b]))
    packed4a = weight_gradient(chain, field, place, pair_in, pair4[0], 0, half, pack, packed)
    held4a = box.send_plane(packed4a)
    packed4b = weight_gradient(chain, field, place, pair_in, pair4[0], half, half, pack, packed)
    held4b = box.send_plane(packed4b)
    kept5, out = box.plane_last(held5)
    held5 = [kept5, box.swap_deep(out)]
    input_grad = input_layer(chain, field, place, weights4, pair4)
    held4a = box.send_second(box.plane_second([held4a]))
    held4b = box.send_second(box.plane_second([held4b]))
    terms = jnp.concatenate([sum4[:, :half], sum4[:, half:], sum5a, sum5b], axis=0)
    kept4a, out = box.plane_last(held4a)
    held4a = [kept4a, box.swap_deep(out)]
    moment5, update5, gram5 = box.finish([held5], conv5_momentum, terms)
    sums5 = box.gram_first(gram5)
    held4b = box.send_deep(box.plane_third(held4b))
    sums5 = box.gram_second(sums5)
    moment4, update4, gram4 = box.finish([held4a, held4b], conv4_momentum, jnp.zeros_like(terms))
    sums4 = box.gram_first(gram4)
    sums5 = box.gram_third(sums5)
    sums4 = box.gram_second(sums4)
    state5 = newton_first(chain, place, box.order, sums5, update5, 2)
    sums4 = box.gram_third(sums4)
    state5 = newton_next(chain, state5, 2, 4)
    new5, copy5 = newton_last(chain, state5, 4, conv5_weight)
    new4, copy4 = newton(chain, place, box.order, sums4, update4, conv4_weight)

    terms = jnp.stack([part[-8] for part in sums5]).reshape(2, 2, half)
    terms = jnp.roll(terms, (place[1], place[2]), axis=(0, 1)).reshape(2, width).T
    grad_bias = lax.dynamic_slice_in_dim(terms, lax.axis_index("dp") * biases.shape[0], biases.shape[0], 0)
    bias_moment = 0.5 * bias_momentum + grad_bias
    bias_new = biases - 0.001 * (grad_bias + 0.5 * bias_moment)
    return (
        field.unflat(jnp.concatenate([out5a, out5b], axis=1)),
        field.unflat(input_grad),
        moment4,
        moment5,
        new4,
        new5,
        copy4,
        copy5,
        bias_moment,
        bias_new,
    )


def on_device(
    frames,
    cotangent,
    clip_counts,
    conv4_weight,
    conv5_weight,
    biases,
    conv4_momentum,
    conv5_momentum,
    bias_momentum,
):
    count, side, width = (frames.shape[0], frames.shape[1], frames.shape[3])
    half = width // 2
    field = Field(side, count)
    place = jnp.zeros((3,), jnp.int32)
    chain = Chain()

    def gather(value):
        return lax.all_gather(value.astype(BF), "dp", axis=0, tiled=True)

    def scatter(value):
        return lax.psum_scatter(value, "dp", scatter_dimension=0, tiled=True)

    def weights(*arrays):
        total = arrays[0].shape[0]
        result = Weights(total)
        for array in arrays:
            result.add(array.shape[1], [(array, 0, 0, total, lambda place: 0)])
        return result

    def keep(place_ref, grad, outs):
        outs[0][...] = grad[...]

    full4, full5 = gather(conv4_weight), gather(conv5_weight)
    bias_block = jnp.pad(gather(biases).T, ((0, BIAS_ROWS - 2), (0, 0)))
    pair_in = field.pair(field.flat(frames))
    mask = (jnp.arange(count, dtype=jnp.int32) < jnp.sum(clip_counts)).astype(BF)
    upstream = field.flat(cotangent * mask[:, None, None, None])
    whole = [((full4.shape[0], half), F32)]
    weights4 = weights(full4)
    weights4.arrays.append(bias_block)
    *pair_mid, slope_mid, bias = first_layer(chain, field, place, weights4, pair_in, [(bias_block, 0)])
    parts = []
    for columns in (slice(0, half), slice(half, width)):
        parts.append(
            second_layer(
                chain, field, place, weights(full5[:, columns]), pair_mid, bias[1:2, columns], upstream[:, columns], keep, whole
            )
        )
    back = [part[1:3] for part in parts]
    *pair4, sum4 = back_layer(chain, field, place, weights(full5[:, :half], full5[:, half:]), back, slope_mid)
    grad5 = scatter(jnp.concatenate([part[4] for part in parts], axis=1))
    grad4 = scatter(
        jnp.concatenate(
            [weight_gradient(chain, field, place, pair_in, pair4[0], at, half, keep, whole)[0] for at in (0, half)], axis=1
        )
    )
    input_grad = input_layer(chain, field, place, weights(full4), pair4)
    grad_bias = scatter(jnp.concatenate([sum4, parts[0][3], parts[1][3]], axis=1).reshape(2, width).T)

    def step(grad, momentum, weight):
        moment = 0.5 * momentum + grad
        update = grad + 0.5 * moment

        def kernel(update_ref, gram_ref):
            gram_into(4, update_ref[...], jnp.zeros((4, half), F32), gram_ref)

        gram = chain.run(kernel, [(VMEM, update)], [((4, width // 4 + 8, half), F32)])[0]
        gram = lax.psum(gram, "dp")
        new, copy = newton(chain, place, lambda place, j: j, [gram[k] for k in range(4)], update, weight)
        return moment, new, copy

    moment4, new4, copy4 = step(grad4, conv4_momentum, conv4_weight)
    moment5, new5, copy5 = step(grad5, conv5_momentum, conv5_weight)
    bias_moment = 0.5 * bias_momentum + grad_bias
    bias_new = biases - 0.001 * (grad_bias + 0.5 * bias_moment)
    return (
        field.unflat(jnp.concatenate([part[0] for part in parts], axis=1)),
        field.unflat(input_grad),
        moment4,
        moment5,
        new4,
        new5,
        copy4,
        copy5,
        bias_moment,
        bias_new,
    )


def solution(mesh):
    n = mesh.shape["dp"]
    rows = P(("stream", "dp"), None)
    field = P(("stream", "dp"), None, None, None)

    def program(*arrays):
        own = arrays[3].shape[0]
        if n % 4 == 0 and n > 4 and own % 32 == 0:
            return on_box(n, *arrays)
        return on_device(*arrays)

    return jax.shard_map(
        program,
        mesh=mesh,
        in_specs=(field, field, P(("stream", "dp")), rows, rows, rows, rows, rows, rows),
        out_specs=(field, field) + (rows,) * 8,
        check_vma=False,
    )
```

```python
import functools
import math

import jax
import jax.numpy as jnp
from jax import lax
from jax.experimental import pallas as pl
from jax.experimental.pallas import tpu as pltpu
from jax.sharding import PartitionSpec as P

NS_STEPS = 5
BIAS_ROWS = 16
BLOCK = 256
LANES = 128
BF = jnp.bfloat16
F32 = jnp.float32
VMEM = pl.BlockSpec(memory_space=pltpu.VMEM)
SMEM = pl.BlockSpec(memory_space=pltpu.SMEM)
ANY = pl.BlockSpec(memory_space=pl.ANY)
HBM = pl.BlockSpec(memory_space=pltpu.HBM)


def together(*values):
    return lax.optimization_barrier(values)


class Chain:
    def __init__(self):
        self.link = None

    def run(self, kernel, operands, outs, scratch=(), limit=20, need=()):
        before = list(need) + ([] if self.link is None else [self.link])
        n, m = len(operands), len(before)

        def linked(*refs):
            link = refs[n + m + len(outs)]
            kernel(*refs[:n], *refs[n + m : n + m + len(outs)], *refs[n + m + len(outs) + 1 :])
            link[...] = jnp.zeros_like(link)

        result = pl.pallas_call(
            linked,
            in_specs=[spec for spec, _ in operands] + [ANY] * m,
            out_specs=[VMEM] * (len(outs) + 1),
            out_shape=[jax.ShapeDtypeStruct(shape, kind) for shape, kind in outs + [((8, 128), F32)]],
            scratch_shapes=list(scratch),
            compiler_params=pltpu.CompilerParams(vmem_limit_bytes=limit * 1024 * 1024),
            cost_estimate=pl.CostEstimate(flops=1, bytes_accessed=100_000, transcendentals=0),
        )(*[array for _, array in operands], *before)
        *results, self.link = result
        return results


def copy_all(pairs, sem):
    copies = [pltpu.make_async_copy(source, target, sem.at[k]) for k, (source, target) in enumerate(pairs)]
    for copy in copies:
        copy.start()
    for copy in copies:
        copy.wait()


class Field:
    def __init__(self, side, count):
        self.side, self.count = side, count
        self.line = (side + 1) * count
        self.cells = side * self.line
        self.lead = -(-self.line // 16) * 16 + 16
        self.rows = -(-(self.lead + self.cells + self.line + count) // 16) * 16

    def tap(self, r, s):
        start = self.lead + (r - 1) * self.line + (s - 1) * self.count
        return (0, start) if start % 16 == 0 else (1, start - self.count)

    def flat(self, values):
        cells = jnp.transpose(values, (1, 2, 0, 3))
        cells = jnp.pad(cells, ((0, 0), (0, 1), (0, 0), (0, 0)))
        return cells.reshape(self.cells, -1)

    def pair(self, flat):
        after = self.rows - self.lead - self.cells
        return (
            jnp.pad(flat, ((self.lead, after), (0, 0))),
            jnp.pad(flat, ((self.lead - self.count, after + self.count), (0, 0))),
        )

    def unflat(self, flat):
        cells = flat.reshape(self.side, self.side + 1, self.count, -1)[:, : self.side]
        return jnp.transpose(cells, (2, 0, 1, 3))

    def sweep(self, wide, pair, columns, body):
        count, lead, line, cells = self.count, self.lead, self.line, self.cells
        width = wide.shape[1]
        pad = jnp.zeros((count, LANES), F32)

        totals = [jnp.zeros((8, LANES), F32)] * (width // LANES)
        for row in range(0, cells, line):
            for c in range(0, width, LANES):
                some = slice(columns.start + c, columns.start + c + LANES)
                value = body(slice(row, row + line), some, wide[row + count : row + count + line, c : c + LANES])
                value = jnp.concatenate([value[: line - count], pad], axis=0)
                low = value.astype(BF)
                pair[0][lead + row : lead + row + line, some] = low
                value = low.astype(F32)
                wide[row + count : row + count + line, c : c + LANES] = value
                totals[c // LANES] = totals[c // LANES] + jnp.sum(value.reshape(line // 8, 8, LANES), axis=0)
        wide[0:count] = jnp.zeros((count, width), F32)
        wide[count + cells :] = jnp.zeros((count, width), F32)
        end = self.rows - lead - cells
        pair[0][0:lead, columns] = jnp.zeros((lead, width), BF)
        pair[0][lead + cells :, columns] = jnp.zeros((end, width), BF)
        pair[1][0 : lead - 16, columns] = jnp.zeros((lead - 16, width), BF)
        pair[1][lead + cells :, columns] = jnp.zeros((end, width), BF)
        pair[1][lead - 16 : lead + cells, columns] = wide[0 : cells + 16, :].astype(BF)
        return jnp.concatenate([jnp.sum(total, axis=0, keepdims=True) for total in totals], axis=1)

    def wide(self):
        return pltpu.VMEM((self.cells + 2 * self.count, BLOCK), F32)


def convolve_block(field, pair, full, columns):
    width = pair[0].shape[1]
    total = None
    for r in range(3):
        for s in range(3):
            which, start = field.tap(r, s)
            tap = (3 * r + s) * width
            part = jnp.dot(
                pair[which][start : start + field.cells, :],
                full[tap : tap + width, columns],
                preferred_element_type=F32,
            )
            total = part if total is None else total + part
    return total


def convolve_back_block(field, pairs, full, at, cols):
    width = full.shape[0] // 9
    total = None
    for r in range(3):
        for s in range(3):
            which, start = field.tap(2 - r, 2 - s)
            tap = (3 * r + s) * width + at
            begin = 0
            for pair in pairs:
                end = begin + pair[0].shape[1]
                part = lax.dot_general(
                    pair[which][start : start + field.cells, :],
                    full[tap : tap + cols, begin:end],
                    (((1,), (1,)), ((), ())),
                    preferred_element_type=F32,
                )
                total = part if total is None else total + part
                begin = end
    return total


def gradient_into(field, pair, delta, out, looped):
    width = pair[0].shape[1]

    def line(r, carry):
        for s in range(3):
            which, start = field.tap(0, s)
            start = start + r * field.line
            tap = (3 * r + s) * width
            if looped:
                start, tap = pl.multiple_of(start, 16), pl.multiple_of(tap, width)
            out[pl.ds(tap, width), :] = lax.dot_general(
                pair[which][pl.ds(start, field.cells), :], delta[...], (((0,), (0,)), ((), ())), preferred_element_type=F32
            )
        return carry

    if looped:
        lax.fori_loop(0, 3, line, 0)
    else:
        for r in range(3):
            line(r, 0)


def activate(value):
    square = value * value
    slope = 0.7978845608
    bend = jnp.tanh(slope * value * (1.0 + 0.044715 * square))
    rise = 0.5 * (1.0 + bend)
    steep = slope * (1.0 + 3 * 0.044715 * square)
    return value * rise, rise + 0.5 * value * (1.0 - bend * bend) * steep


class Weights:
    def __init__(self, total):
        self.total, self.cols = total, 0
        self.arrays, self.plan = [], []

    def add(self, cols, found):
        for part, start, left, height, where in found:
            if not any(other is part for other in self.arrays):
                self.arrays.append(part)
            which = [k for k, other in enumerate(self.arrays) if other is part][0]
            self.plan.append((which, start, left, height, where, self.cols, cols))
        self.cols += cols
        return self

    def operands(self):
        return [(HBM, array) for array in self.arrays]

    def scratch(self, more=0):
        return [pltpu.VMEM((self.total, self.cols), BF), pltpu.SemaphoreType.DMA((len(self.plan) + more,))]

    def copies(self, place, arrays, full):
        return [
            (
                arrays[which].at[pl.ds(start, height), pl.ds(left, cols)],
                full.at[pl.ds(pl.multiple_of(where(place), 16), height), pl.ds(column, cols)],
            )
            for which, start, left, height, where, column, cols in self.plan
        ]


def first_layer(chain, field, place, weights, pair, bias):
    width = weights.cols
    n = len(weights.arrays)
    def kernel(*refs):
        place_ref, arrays, rest = refs[0], refs[1 : n + 1], refs[n + 1 :]
        even_in, odd_in, bias_ref, out_even, out_odd, slope_ref, even, odd, wide, full, sem = rest
        copy_all(weights.copies(place_ref, arrays, full) + [(even_in, even), (odd_in, odd)], sem)
        for at in range(0, width, BLOCK):
            columns = slice(at, at + BLOCK)
            wide[field.count : field.count + field.cells] = convolve_block(field, (even, odd), full, columns)

            def body(rows, some, value):
                result, slope_ref[rows, some] = activate(value + bias_ref[0:1, some])
                return result

            field.sweep(wide, (out_even, out_odd), columns, body)

    form = pltpu.VMEM(pair[0].shape, BF)
    return chain.run(
        kernel,
        [(SMEM, place)] + weights.operands() + [(HBM, pair[0]), (HBM, pair[1]), (VMEM, bias)],
        [((field.rows, width), BF)] * 2 + [((field.cells, width), F32)],
        [form, form, field.wide()] + weights.scratch(2),
        limit=54,
    )


def second_layer(chain, field, place, weights, pair, bias, upstream, pack, packed, need=()):
    width = weights.cols
    n = len(weights.arrays)

    def kernel(*refs):
        place_ref, arrays, rest = refs[0], refs[1 : n + 1], refs[n + 1 :]
        even, odd, bias_ref, up_in, out_ref, d_even, d_odd, sum_ref, *outs, grad, up_ref, wide, full, sem = rest
        copy_all(weights.copies(place_ref, arrays, full) + [(up_in, up_ref)], sem)
        wide[field.count : field.count + field.cells] = convolve_block(field, (even, odd), full, slice(0, width))

        def body(rows, some, value):
            result, slope = activate(value + bias_ref[:, some])
            out_ref[rows, some] = result.astype(BF)
            return up_ref[rows, some].astype(F32) * slope

        sum_ref[...] = field.sweep(wide, (d_even, d_odd), slice(0, width), body)
        gradient_into(field, (even, odd), d_even.at[pl.ds(field.lead, field.cells)], grad, True)
        pack(place_ref, grad, outs)

    form = ((field.rows, width), BF)
    return chain.run(
        kernel,
        [(SMEM, place)] + weights.operands() + [(VMEM, pair[0]), (VMEM, pair[1]), (VMEM, bias), (HBM, upstream)],
        [((field.cells, width), BF), form, form, ((1, width), F32)] + packed,
        [pltpu.VMEM((9 * pair[0].shape[1], width), F32), pltpu.VMEM((field.cells, width), BF)]
        + [field.wide()]
        + weights.scratch(1),
        limit=24,
        need=need,
    )


def back_layer(chain, field, place, weights, pairs, slope, need=()):
    width = weights.total // 9
    n = len(weights.arrays)
    flat = [form for pair in pairs for form in pair]

    def kernel(*refs):
        place_ref, arrays, rest = refs[0], refs[1 : n + 1], refs[n + 1 :]
        deltas, rest = rest[: len(flat)], rest[len(flat) :]
        slope_in, d_even, d_odd, sum_ref, slope_ref, wide, full, sem = rest
        copy_all(weights.copies(place_ref, arrays, full) + [(slope_in, slope_ref)], sem)
        held = [deltas[k : k + 2] for k in range(0, len(flat), 2)]
        for at in range(0, width, BLOCK):
            columns = slice(at, at + BLOCK)
            wide[field.count : field.count + field.cells] = convolve_back_block(field, held, full, at, BLOCK)

            def body(rows, some, value):
                return value * slope_ref[rows, some]

            sum_ref[:, columns] = field.sweep(wide, (d_even, d_odd), columns, body)

    return chain.run(
        kernel,
        [(SMEM, place)] + weights.operands() + [(VMEM, form) for form in flat] + [(HBM, slope)],
        [((field.rows, width), BF)] * 2 + [((1, width), F32)],
        [pltpu.VMEM(slope.shape, F32), field.wide()]
        + weights.scratch(1),
        limit=24,
        need=need,
    )


def input_layer(chain, field, place, weights, pair):
    n = len(weights.arrays)
    width = weights.total // 9

    def kernel(*refs):
        place_ref, arrays, rest = refs[0], refs[1 : n + 1], refs[n + 1 :]
        even_in, odd_in, out_ref, even, odd, full, sem = rest
        copy_all(weights.copies(place_ref, arrays, full) + [(even_in, even), (odd_in, odd)], sem)
        for at in range(0, width, BLOCK):
            out_ref[:, at : at + BLOCK] = convolve_back_block(field, [(even, odd)], full, at, BLOCK).astype(BF)

    operands = [(SMEM, place)] + weights.operands() + [(ANY, pair[0]), (ANY, pair[1])]
    form = pltpu.VMEM(pair[0].shape, BF)
    return chain.run(kernel, operands, [((field.cells, width), BF)], [form, form] + weights.scratch(2), limit=54)[0]


def weight_gradient(chain, field, place, pair, delta, at, cols, pack, packed, need=()):
    width = pair[0].shape[1]

    def kernel(place_ref, even_in, odd_in, delta_ref, *rest):
        *outs, even, odd, grad, sem = rest
        copy_all([(even_in, even), (odd_in, odd)], sem)
        delta = delta_ref.at[pl.ds(field.lead, field.cells), pl.ds(at, cols)]
        gradient_into(field, (even, odd), delta, grad, False)
        pack(place_ref, grad, outs)

    form = pltpu.VMEM(pair[0].shape, BF)
    return chain.run(
        kernel,
        [(SMEM, place), (HBM, pair[0]), (HBM, pair[1]), (VMEM, delta)],
        packed,
        [form, form, pltpu.VMEM((9 * width, cols), F32), pltpu.SemaphoreType.DMA((2,))],
        limit=20,
        need=need,
    )


def halves(value):
    high = value.astype(BF)
    return high, (value - high.astype(F32)).astype(BF)


def product(left, right):
    return jnp.dot(
        jnp.concatenate([left[0], left[0], left[1]], axis=1),
        jnp.concatenate([right[0], right[1], right[0]], axis=0),
        preferred_element_type=F32,
    )


def square_masks(size):
    row = lax.broadcasted_iota(jnp.int32, (size, size), 0)
    column = lax.broadcasted_iota(jnp.int32, (size, size), 1)
    return row, column


def gram_into(parts, update, terms, out_ref):
    low = update.astype(BF)
    half = low.shape[1] // 2
    each = 2 * half // parts
    left, right = low[:, :half], low[:, half:]

    def block(one, two):
        return lax.dot_general(one, two, (((0,), (0,)), ((), ())), preferred_element_type=F32)

    row, column = square_masks(half)
    last = block(right, right)
    for k, value in enumerate((block(left, right), jnp.where(column >= row, block(left, left), last))):
        for part in range(parts):
            first = max(part * each, k * half)
            end = min((part + 1) * each, (k + 1) * half)
            if first < end:
                out_ref[part, first - part * each : end - part * each] = value[first - k * half : end - k * half]
    diagonal = jnp.sum(jnp.where(column == row, last, 0.0), axis=0, keepdims=True)
    for part in range(parts):
        out_ref[part, each : each + 1] = terms[part : part + 1]
        out_ref[part, each + 1 : each + 2] = diagonal if part == 0 else jnp.zeros_like(diagonal)
        out_ref[part, each + 2 :] = jnp.zeros((6, half), F32)


def newton_start(order, place_ref, sums, update_ref, packed, below):
    each = packed.shape[0] // len(sums)
    for j, part in enumerate(sums):
        at = order(place_ref, j)
        packed[pl.ds(pl.multiple_of(at * each, 8), each), :] = part[:each]
        below[pl.ds(pl.multiple_of(at * 8, 8), 8), :] = part[each:]
    half = packed.shape[1]
    row, column = square_masks(half)
    corner = packed[:half]
    mixed = packed[half:]
    turned = mixed.T
    last = jnp.where(column < row, mixed, jnp.where(column > row, turned, below[1:2]))
    gram = jnp.concatenate(
        [
            jnp.concatenate([jnp.where(column >= row, mixed, turned), corner], axis=1),
            jnp.concatenate([corner.T, last], axis=1),
        ],
        axis=0,
    )
    square = jnp.sum(jnp.where(column == row, mixed, 0.0)) + jnp.sum(below[1:2])
    scale = 1.0 / (jnp.sqrt(square) + 1e-07)
    return gram * scale * scale, update_ref[...] * scale


def newton_steps(gram, iterate, steps):
    for step in steps:
        parts = halves(gram)
        poly = halves(-4.775 * gram + 2.0315 * product(parts, parts))
        iterate = 3.4445 * iterate + product(halves(iterate), poly)
        if step < NS_STEPS - 1:
            middle = 3.4445 * gram + product(parts, poly)
            gram = 3.4445 * middle + product(halves(middle), poly)
    return gram, iterate


def newton(chain, place, order, sums, update, weight):
    width = weight.shape[1]
    n = len(sums)

    def kernel(place_ref, *refs):
        update_ref, weight_ref, new_ref, copy_ref, packed, below = refs[n:]
        state = newton_start(order, place_ref, refs[:n], update_ref, packed, below)
        new = weight_ref[...] - newton_steps(*state, range(NS_STEPS))[1]
        new_ref[...] = new
        copy_ref[...] = new.astype(BF)

    return chain.run(
        kernel,
        [(SMEM, place)] + [(VMEM, part) for part in sums] + [(VMEM, update), (VMEM, weight)],
        [(weight.shape, F32), (weight.shape, BF)],
        [pltpu.VMEM((width, width // 2), F32), pltpu.VMEM((8 * n, width // 2), F32)],
    )


def newton_first(chain, place, order, sums, update, last):
    width = update.shape[1]
    n = len(sums)

    def kernel(place_ref, *refs):
        update_ref, gram_ref, iterate_ref, packed, below = refs[n:]
        state = newton_start(order, place_ref, refs[:n], update_ref, packed, below)
        gram_ref[...], iterate_ref[...] = newton_steps(*state, range(last))

    return chain.run(
        kernel,
        [(SMEM, place)] + [(VMEM, part) for part in sums] + [(VMEM, update)],
        [((width, width), F32), (update.shape, F32)],
        [pltpu.VMEM((width, width // 2), F32), pltpu.VMEM((8 * n, width // 2), F32)],
    )


def newton_next(chain, state, first, last):
    def kernel(gram_ref, iterate_ref, gram_out, iterate_out):
        gram_out[...], iterate_out[...] = newton_steps(gram_ref[...], iterate_ref[...], range(first, last))

    return chain.run(kernel, [(VMEM, part) for part in state], [(part.shape, F32) for part in state])


def newton_last(chain, state, first, weight):
    def kernel(gram_ref, iterate_ref, weight_ref, new_ref, copy_ref):
        new = weight_ref[...] - newton_steps(gram_ref[...], iterate_ref[...], range(first, NS_STEPS))[1]
        new_ref[...] = new
        copy_ref[...] = new.astype(BF)

    operands = [(VMEM, part) for part in state] + [(VMEM, weight)]
    return chain.run(kernel, operands, [(weight.shape, F32), (weight.shape, BF)])


class Box:
    def __init__(self, chain, n, rows):
        self.chain = chain
        self.depth = n // 4
        self.n, self.rows, self.cut = n, rows, rows // 2
        me = lax.axis_index("dp")
        self.place = jnp.stack([me // 4, me // 2 % 2, me % 2]).astype(jnp.int32)

    def move(self, block, z, y=0, x=0):
        pairs = []
        for index in range(self.n):
            to = ((index // 4 + z) % self.depth) * 4 + ((index // 2 + y) % 2) * 2 + (index + x) % 2
            pairs.append((index, to))
        return lax.ppermute(block, "dp", pairs)

    def deep(self, block):
        return [self.move(block, -j) for j in range(1, self.depth)]

    def swap_deep(self, blocks):
        groups = [[4 * z + k for z in range(self.depth)] for k in range(4)]
        return lax.all_to_all(blocks, "dp", 0, 0, axis_index_groups=groups, tiled=True)

    def owner(self, z, y, x, fixed):
        def where(place):
            at = z if fixed else lax.rem(place[0] + z, self.depth)
            return ((at * 2 + lax.rem(place[1] + y, 2)) * 2 + lax.rem(place[2] + x, 2)) * self.rows

        return where


    def split(self, blocks, parts):
        cut, low = self.cut, blocks[0].shape[0] - self.cut
        cols = blocks[0].shape[1] // parts

        def kernel(*refs):
            sources, outs = refs[: len(blocks)], refs[len(blocks) :]
            for k in range(parts):
                columns = slice(k * cols, (k + 1) * cols)
                for j, source in enumerate(sources):
                    outs[2 * k][j * cut : (j + 1) * cut] = source[:cut, columns]
                    outs[2 * k + 1][j * low : (j + 1) * low] = source[cut:, columns]

        outs = [((len(blocks) * cut, cols), BF), ((len(blocks) * low, cols), BF)] * parts
        return self.chain.run(kernel, [(VMEM, block) for block in blocks], outs)

    def swap_plane(self, blocks):
        groups = [[4 * z + k for k in range(4)] for z in range(self.depth)]
        return lax.all_to_all(blocks, "dp", 0, 0, axis_index_groups=groups, tiled=True)

    def add_rows(self, blocks, came, copies, kind):
        tall, cols = blocks.shape[0] // came, blocks.shape[1]

        def kernel(source, out):
            total = source[0:tall].astype(F32)
            for k in range(1, came):
                total = total + source[k * tall : (k + 1) * tall].astype(F32)
            for k in range(copies):
                out[k * tall : (k + 1) * tall] = total.astype(kind)

        return self.chain.run(kernel, [(VMEM, blocks)], [((copies * tall, cols), kind)])[0]

    def gate(self, arrays):
        def kernel(out):
            out[...] = jnp.zeros_like(out)

        self.chain.run(kernel, [], [((8, 128), F32)], need=arrays)

    def near(self, blocks, need=()):
        cut, tall = self.cut, blocks[0].shape[0]
        low = tall - cut

        def kernel(*refs):
            *sources, upper, lower = refs
            for j, source in enumerate(sources):
                upper[j * cut : (j + 1) * cut] = source[:cut]
                lower[j * low : (j + 1) * low] = source[cut:]

        cols = blocks[0].shape[1]
        outs = [((len(blocks) * cut, cols), BF), ((len(blocks) * low, cols), BF)]
        return self.chain.run(kernel, [(VMEM, block) for block in blocks], outs, need=need)

    def found(self, upper, lower, tall, fixed=False):
        pieces = []
        for at, height, arrays in ((0, tall[0], upper), (self.cut, tall[1], lower)):
            for (y, x), array, first in arrays:
                for z in range(self.depth):
                    where = functools.partial(lambda f, a, p: f(p) + a, self.owner(z, y, x, fixed), at)
                    pieces.append((array, first + z * height // self.depth, 0, self.cut, where))
        return pieces

    def gather_planes(self, upper, lower, x_upper, y_lower, need=()):
        tall = upper.shape[0], lower.shape[0]
        cols = upper.shape[1]

        def kernel(a, a_got, b, b_got, a_wide, b_wide):
            a_wide[: tall[0]], a_wide[tall[0] :] = a[...], a_got[...]
            b_wide[: tall[1]], b_wide[tall[1] :] = b[...], b_got[...]

        operands = [(VMEM, array) for array in (upper, x_upper, lower, y_lower)]
        wide = self.chain.run(kernel, operands, [((2 * height, cols), BF) for height in tall], need=need)
        y_wide, x_wide = self.move(wide[0], 0, 1, 0), self.move(wide[1], 0, 0, 1)
        uppers = [((0, 0), wide[0], 0), ((0, 1), wide[0], tall[0]), ((1, 0), y_wide, 0), ((1, 1), y_wide, tall[0])]
        lowers = [((0, 0), wide[1], 0), ((1, 0), wide[1], tall[1]), ((0, 1), x_wide, 0), ((1, 1), x_wide, tall[1])]
        return uppers, lowers, tall


    def block(self, ref, index, rows):
        return ref[pl.ds(pl.multiple_of(index * rows, 8), rows), :]

    def packed_plane(self, cols):
        tall = 2 * self.depth * self.cut
        return [((tall, cols), BF)] * 4

    def pack_plane(self, place, grad, outs):
        cut = self.cut
        for z in range(self.depth):
            for k in range(2):
                to = slice((2 * z + k) * cut, (2 * z + k + 1) * cut)
                for step in range(2):
                    x = lax.rem(place[2] + step, 2)
                    y = lax.rem(place[1] + step, 2)
                    upper = ((z * 2 + k) * 2 + x) * self.rows
                    lower = ((z * 2 + y) * 2 + k) * self.rows + cut
                    outs[step][to] = grad[pl.ds(pl.multiple_of(upper, 8), cut), :].astype(BF)
                    outs[2 + step][to] = grad[pl.ds(pl.multiple_of(lower, 8), cut), :].astype(BF)

    def send_plane(self, packed):
        return [packed[0], self.move(packed[1], 0, 0, 1), packed[2], self.move(packed[3], 0, 1, 0)]

    def plane_second(self, chunks, need=()):
        cut, depth = self.cut, self.depth
        flat = [part for held in chunks for part in held]

        def kernel(place, *refs):
            a_keep, a_out, b_keep, b_out = refs[len(flat) :]
            column = 0
            for k in range(0, len(flat), 4):
                a, a_got, b, b_got = refs[k : k + 4]
                columns = slice(column, column + a.shape[1])
                column += a.shape[1]
                for z in range(depth):
                    to = slice(z * cut, (z + 1) * cut)
                    for step in range(2):
                        y = 2 * z + lax.rem(place[1] + step, 2)
                        x = 2 * z + lax.rem(place[2] + step, 2)
                        upper = self.block(a, y, cut).astype(F32) + self.block(a_got, y, cut).astype(F32)
                        lower = self.block(b, x, cut).astype(F32) + self.block(b_got, x, cut).astype(F32)
                        if step == 0:
                            a_keep[to, columns], b_keep[to, columns] = upper, lower
                        else:
                            a_out[to, columns], b_out[to, columns] = upper.astype(BF), lower.astype(BF)

        cols = sum(held[0].shape[1] for held in chunks)
        outs = [((depth * cut, cols), kind) for kind in (F32, BF, F32, BF)]
        return self.chain.run(kernel, [(SMEM, self.place)] + [(VMEM, part) for part in flat], outs, need=need)

    def send_second(self, packed):
        return [packed[0], self.move(packed[1], 0, 1, 0), packed[2], self.move(packed[3], 0, 0, 1)]

    def plane_third(self, held):
        cut, depth = self.cut, self.depth

        def kernel(place, a, a_got, b, b_got, keep, *outs):
            for step in range(depth):
                z = lax.rem(place[0] + step, depth)
                upper = self.block(a, z, cut) + self.block(a_got, z, cut).astype(F32)
                lower = self.block(b, z, cut) + self.block(b_got, z, cut).astype(F32)
                if step == 0:
                    keep[:cut], keep[cut:] = upper, lower
                else:
                    outs[step - 1][:cut], outs[step - 1][cut:] = upper.astype(BF), lower.astype(BF)

        cols = held[0].shape[1]
        outs = [((self.rows, cols), kind) for kind in [F32] + [BF] * (depth - 1)]
        return self.chain.run(kernel, [(SMEM, self.place)] + [(VMEM, part) for part in held], outs)

    def plane_last(self, held):
        cut, depth, rows = self.cut, self.depth, self.rows

        def kernel(place, a, a_got, b, b_got, keep, out):
            for step in range(depth):
                z = lax.rem(place[0] + step, depth)
                upper = self.block(a, z, cut) + self.block(a_got, z, cut).astype(F32)
                lower = self.block(b, z, cut) + self.block(b_got, z, cut).astype(F32)
                if step == 0:
                    keep[:cut], keep[cut:] = upper, lower
                    upper, lower = jnp.zeros_like(upper), jnp.zeros_like(lower)
                out[pl.ds(pl.multiple_of(z * rows, 16), cut), :] = upper.astype(BF)
                out[pl.ds(pl.multiple_of(z * rows + cut, 16), rows - cut), :] = lower.astype(BF)

        cols = held[0].shape[1]
        outs = [((rows, cols), F32), ((depth * rows, cols), BF)]
        return self.chain.run(kernel, [(SMEM, self.place)] + [(VMEM, part) for part in held], outs)

    def send_deep(self, packed):
        return [packed[0]] + [self.move(part, j + 1) for j, part in enumerate(packed[1:])]

    def finish(self, chunks, momentum, terms):
        flat = [part for parts in chunks for part in parts]
        width = momentum.shape[1]
        each = width // 4

        def kernel(*refs):
            sources, (momentum_ref, terms_ref, moment, update, gram) = refs[: len(flat)], refs[len(flat) :]
            at = column = 0
            for parts in chunks:
                total = sources[at][...]
                for part in sources[at + 1 : at + len(parts)]:
                    for row in range(0, part.shape[0], self.rows):
                        total = total + part[row : row + self.rows].astype(F32)
                at += len(parts)
                columns = slice(column, column + total.shape[1])
                column += total.shape[1]
                value = 0.5 * momentum_ref[:, columns] + total
                moment[:, columns] = value
                update[:, columns] = total + 0.5 * value
            gram_into(4, update[...], terms_ref[...], gram)

        outs = [(momentum.shape, F32)] * 2 + [((4, each + 8, width // 2), F32)]
        operands = [(VMEM, part) for part in flat] + [(VMEM, momentum), (VMEM, terms)]
        return self.chain.run(kernel, operands, outs)


    PLANES = ((0, 1), (1, 0), (1, 1))

    def gram_first(self, parts):
        each, half = parts.shape[1:]

        def kernel(place, parts_ref, *outs):
            for (y, x), out in zip(((0, 0),) + self.PLANES, outs):
                at = lax.rem(place[1] + y, 2) * 2 + lax.rem(place[2] + x, 2)
                out[...] = parts_ref[at]

        packed = self.chain.run(kernel, [(SMEM, self.place), (VMEM, parts)], [((each, half), F32)] * 4)
        return [packed[0]] + [self.move(part, 0, *at) for part, at in zip(packed[1:], self.PLANES)]

    def add(self, parts):
        def kernel(*refs):
            total = refs[0][...]
            for part in refs[1:-1]:
                total = total + part[...]
            refs[-1][...] = total

        return self.chain.run(kernel, [(VMEM, part) for part in parts], [(parts[0].shape, F32)])[0]

    def gram_second(self, got):
        own = self.add(got)
        return [own] + self.deep(own)

    def gram_third(self, got):
        own = self.add(got)
        return [own] + [self.move(own, 0, *at) for at in self.PLANES]

    def order(self, place, j):
        return lax.rem(place[1] + j // 2, 2) * 2 + lax.rem(place[2] + j % 2, 2)


def on_box(
    n_dp,
    frames,
    cotangent,
    clip_counts,
    conv4_weight,
    conv5_weight,
    biases,
    conv4_momentum,
    conv5_momentum,
    bias_momentum,
):
    count, side, width = (frames.shape[0], frames.shape[1], frames.shape[3])
    half = width // 2
    rows = conv4_weight.shape[0]
    chain = Chain()
    box = Box(chain, n_dp, rows)
    place = box.place
    field = Field(side, count)
    low4 = conv4_weight.astype(BF)
    low5 = conv5_weight.astype(BF)
    lane = jnp.arange(width, dtype=jnp.int32) // biases.shape[0]
    own = jnp.tile(biases.astype(BF).T, (1, n_dp))
    extra = jnp.where(lane == lax.axis_index("dp"), own, jnp.zeros_like(own))
    extra = jnp.concatenate([extra, jnp.zeros((BIAS_ROWS - 2, width), BF)], axis=0)
    deep4 = box.deep(low4)
    pair_in = field.pair(field.flat(frames))
    mask = (jnp.arange(count, dtype=jnp.int32) < jnp.sum(clip_counts)).astype(BF)
    upstream = field.flat(cotangent * mask[:, None, None, None])
    upstream_a, upstream_b = upstream[:, :half], upstream[:, half:]
    upper4, lower4 = box.near([low4] + deep4, [*pair_in, upstream_a, upstream_b])
    x_upper4, y_lower4 = box.move(upper4, 0, 0, 1), box.move(lower4, 0, 1, 0)
    bias = box.add_rows(box.swap_plane(jnp.concatenate([extra] * 4, axis=0)), 4, box.depth, BF)
    all4 = box.gather_planes(upper4, lower4, x_upper4, y_lower4)
    bias = box.add_rows(box.swap_deep(bias), box.depth, 1, F32)
    upper5a, lower5a, upper5b, lower5b = box.split([low5] + box.deep(low5), 2)
    x_upper5a, y_lower5a = box.move(upper5a, 0, 0, 1), box.move(lower5a, 0, 1, 0)
    x_upper5b, y_lower5b = box.move(upper5b, 0, 0, 1), box.move(lower5b, 0, 1, 0)
    box.gate([all4[0][2][1], all4[1][2][1]])
    all5a = box.gather_planes(upper5a, lower5a, x_upper5a, y_lower5a)

    weights4 = Weights(n_dp * rows).add(width, box.found(*all4))
    *pair_mid, slope_mid = first_layer(chain, field, place, weights4, pair_in, bias)
    all5b = box.gather_planes(
        upper5b, lower5b, x_upper5b, y_lower5b, [all5a[0][2][1], all5a[1][2][1]]
    )
    found5a, found5b = box.found(*all5a), box.found(*all5b)
    pack, packed = box.pack_plane, box.packed_plane(half)

    weights5a = Weights(n_dp * rows).add(half, found5a)
    layer = second_layer(
        chain, field, place, weights5a, pair_mid, bias[1:2, :half], upstream_a, pack, packed
    )
    out5a, pair5a, sum5a, packed5a = layer[0], layer[1:3], layer[3], layer[4:]
    held5a = box.send_plane(packed5a)
    weights5b = Weights(n_dp * rows).add(half, found5b)
    layer = second_layer(
        chain, field, place, weights5b, pair_mid, bias[1:2, half:], upstream_b, pack, packed
    )
    out5b, pair5b, sum5b, packed5b = layer[0], layer[1:3], layer[3], layer[4:]
    held5b = box.send_plane(packed5b)
    weights5 = Weights(n_dp * rows).add(half, found5a).add(half, found5b)
    *pair4, sum4 = back_layer(chain, field, place, weights5, [pair5a, pair5b], slope_mid)
    held5 = box.send_second(box.plane_second([held5a, held5b]))
    packed4a = weight_gradient(chain, field, place, pair_in, pair4[0], 0, half, pack, packed)
    held4a = box.send_plane(packed4a)
    packed4b = weight_gradient(chain, field, place, pair_in, pair4[0], half, half, pack, packed)
    held4b = box.send_plane(packed4b)
    kept5, out = box.plane_last(held5)
    held5 = [kept5, box.swap_deep(out)]
    input_grad = input_layer(chain, field, place, weights4, pair4)
    held4a = box.send_second(box.plane_second([held4a]))
    held4b = box.send_second(box.plane_second([held4b]))
    terms = jnp.concatenate([sum4[:, :half], sum4[:, half:], sum5a, sum5b], axis=0)
    kept4a, out = box.plane_last(held4a)
    held4a = [kept4a, box.swap_deep(out)]
    moment5, update5, gram5 = box.finish([held5], conv5_momentum, terms)
    sums5 = box.gram_first(gram5)
    held4b = box.send_deep(box.plane_third(held4b))
    sums5 = box.gram_second(sums5)
    moment4, update4, gram4 = box.finish([held4a, held4b], conv4_momentum, jnp.zeros_like(terms))
    sums4 = box.gram_first(gram4)
    sums5 = box.gram_third(sums5)
    sums4 = box.gram_second(sums4)
    state5 = newton_first(chain, place, box.order, sums5, update5, 2)
    sums4 = box.gram_third(sums4)
    state5 = newton_next(chain, state5, 2, 4)
    new5, copy5 = newton_last(chain, state5, 4, conv5_weight)
    new4, copy4 = newton(chain, place, box.order, sums4, update4, conv4_weight)

    terms = jnp.stack([part[-8] for part in sums5]).reshape(2, 2, half)
    terms = jnp.roll(terms, (place[1], place[2]), axis=(0, 1)).reshape(2, width).T
    grad_bias = lax.dynamic_slice_in_dim(terms, lax.axis_index("dp") * biases.shape[0], biases.shape[0], 0)
    bias_moment = 0.5 * bias_momentum + grad_bias
    bias_new = biases - 0.001 * (grad_bias + 0.5 * bias_moment)
    return (
        field.unflat(jnp.concatenate([out5a, out5b], axis=1)),
        field.unflat(input_grad),
        moment4,
        moment5,
        new4,
        new5,
        copy4,
        copy5,
        bias_moment,
        bias_new,
    )


def on_device(
    frames,
    cotangent,
    clip_counts,
    conv4_weight,
    conv5_weight,
    biases,
    conv4_momentum,
    conv5_momentum,
    bias_momentum,
):
    count, side, width = (frames.shape[0], frames.shape[1], frames.shape[3])
    half = width // 2
    field = Field(side, count)
    place = jnp.zeros((3,), jnp.int32)
    chain = Chain()

    def gather(value):
        return lax.all_gather(value.astype(BF), "dp", axis=0, tiled=True)

    def scatter(value):
        return lax.psum_scatter(value, "dp", scatter_dimension=0, tiled=True)

    def weights(*arrays):
        total = arrays[0].shape[0]
        result = Weights(total)
        for array in arrays:
            result.add(array.shape[1], [(array, 0, 0, total, lambda place: 0)])
        return result

    def keep(place_ref, grad, outs):
        outs[0][...] = grad[...]

    full4, full5 = gather(conv4_weight), gather(conv5_weight)
    bias = jnp.pad(gather(biases).T.astype(F32), ((0, BIAS_ROWS - 2), (0, 0)))
    pair_in = field.pair(field.flat(frames))
    mask = (jnp.arange(count, dtype=jnp.int32) < jnp.sum(clip_counts)).astype(BF)
    upstream = field.flat(cotangent * mask[:, None, None, None])
    whole = [((full4.shape[0], half), F32)]
    weights4 = weights(full4)
    *pair_mid, slope_mid = first_layer(chain, field, place, weights4, pair_in, bias)
    parts = []
    for columns in (slice(0, half), slice(half, width)):
        parts.append(
            second_layer(
                chain, field, place, weights(full5[:, columns]), pair_mid, bias[1:2, columns], upstream[:, columns], keep, whole
            )
        )
    back = [part[1:3] for part in parts]
    *pair4, sum4 = back_layer(chain, field, place, weights(full5[:, :half], full5[:, half:]), back, slope_mid)
    grad5 = scatter(jnp.concatenate([part[4] for part in parts], axis=1))
    grad4 = scatter(
        jnp.concatenate(
            [weight_gradient(chain, field, place, pair_in, pair4[0], at, half, keep, whole)[0] for at in (0, half)], axis=1
        )
    )
    input_grad = input_layer(chain, field, place, weights(full4), pair4)
    grad_bias = scatter(jnp.concatenate([sum4, parts[0][3], parts[1][3]], axis=1).reshape(2, width).T)

    def step(grad, momentum, weight):
        moment = 0.5 * momentum + grad
        update = grad + 0.5 * moment

        def kernel(update_ref, gram_ref):
            gram_into(4, update_ref[...], jnp.zeros((4, half), F32), gram_ref)

        gram = chain.run(kernel, [(VMEM, update)], [((4, width // 4 + 8, half), F32)])[0]
        gram = lax.psum(gram, "dp")
        new, copy = newton(chain, place, lambda place, j: j, [gram[k] for k in range(4)], update, weight)
        return moment, new, copy

    moment4, new4, copy4 = step(grad4, conv4_momentum, conv4_weight)
    moment5, new5, copy5 = step(grad5, conv5_momentum, conv5_weight)
    bias_moment = 0.5 * bias_momentum + grad_bias
    bias_new = biases - 0.001 * (grad_bias + 0.5 * bias_moment)
    return (
        field.unflat(jnp.concatenate([part[0] for part in parts], axis=1)),
        field.unflat(input_grad),
        moment4,
        moment5,
        new4,
        new5,
        copy4,
        copy5,
        bias_moment,
        bias_new,
    )


def solution(mesh):
    n = mesh.shape["dp"]
    rows = P(("stream", "dp"), None)
    field = P(("stream", "dp"), None, None, None)

    def program(*arrays):
        own = arrays[3].shape[0]
        if n % 4 == 0 and n > 4 and own % 32 == 0:
            return on_box(n, *arrays)
        return on_device(*arrays)

    return jax.shard_map(
        program,
        mesh=mesh,
        in_specs=(field, field, P(("stream", "dp")), rows, rows, rows, rows, rows, rows),
        out_specs=(field, field) + (rows,) * 8,
        check_vma=False,
    )
```
